128 devices in a mesh: rows: 32 (over z, y, core), cent: 4 (over x).
Axes of the slice: x: 4, y: 4, z: 4, core: 2. Of those that a mesh axis runs over, the one named last changes fastest.
Arguments:
- embeddings: float32 [262144, 256], P(('rows', 'cent')), may hold values from -6 to 6
- centroids: float32 [8192, 256], P('cent'), may hold values from -6 to 6
- owners: int32 [2048], P(('rows', 'cent')), may hold values from 0 to 31, as said below
- live_blocks: int32 [128], P(('rows', 'cent')), may hold values from 9 to 16
Outputs:
- moved: bfloat16 [524288, 256], P(('rows', 'cent'))
- moved_score: bfloat16 [524288], P(('rows', 'cent'))
- balance: float32 [8192], replicated
The draws below stay inside these ranges and needn't reach their ends.
Inputs may be any that keep to these rules, and one draw needn't show every extreme that they name: `owners`: within one device the blocks name each owner at most 1 times; in each cent group one owner is named exactly 1 times by the live blocks of every device.
All inputs are finite; a program needn't handle non-finite values.
Results may differ from the reference program's by a relative error of at most 0.0041.
Values may be sent and summed in bfloat16 or wider, within the bound.
No kernel may reach another device: no remote copies, remote signals or barrier semaphores. Data moves between devices by JAX's collectives and lax.ppermute only.
A program may use at most 64 MiB of HBM per device.

```python
import math
import jax
import jax.numpy as jnp
from jax import lax

D = 256
CENTS = 8192
BLOCK_ROWS = 128
BLK = 16
ITERS = 1
NROWS = 262144
BLOCKS = 2048
SLOT = 1
N_ROWS = 32
N_CENT = 4


def draw_owners(key, part):
    key = jax.random.fold_in(key, 11)
    devices = BLOCKS // BLK
    slots_all = N_ROWS * SLOT
    half_blocks = BLK // 2
    hot_owner = jax.random.randint(jax.random.fold_in(key, 1), (N_CENT,), 0, N_ROWS)
    device_keys = jax.random.split(jax.random.fold_in(key, 2), devices)
    identity = jnp.arange(slots_all, dtype=jnp.int32)

    def per_device(device_key, device_hot):
        first_key, second_key = jax.random.split(device_key)
        priority = jax.random.permutation(first_key, slots_all).astype(jnp.int32)
        is_hot = identity % N_ROWS == device_hot
        priority = jnp.where(is_hot, -1 - identity, priority)
        ranking = jnp.argsort(priority, stable=True)
        chosen = ranking[:BLK]
        shuffled = jax.random.permutation(second_key, half_blocks)
        front_part = chosen[:half_blocks][shuffled]
        return (jnp.concatenate([front_part, chosen[half_blocks:]]) % N_ROWS).astype(jnp.int32)
    device_hot = hot_owner[jnp.arange(devices) % N_CENT]
    return jax.vmap(per_device)(device_keys, device_hot).reshape(-1)


def draw_live_blocks(key, part):
    key = jax.random.fold_in(key, 23)
    devices = BLOCKS // BLK
    lowest = BLK // 2 + 1
    counts = jax.random.randint(jax.random.fold_in(key, 1), (devices,), lowest, BLK + 1)
    chosen_devices = jax.random.permutation(jax.random.fold_in(key, 2), devices)
    counts = counts.at[chosen_devices[0]].set(BLK).at[chosen_devices[1]].set(lowest)
    return counts.astype(jnp.int32)


def shard_levels(stream_key, extent, pieces, smallest, largest):
    gain = 1.0
    for dim, blocks in pieces:
        steps = jax.random.uniform(jax.random.fold_in(jax.random.fold_in(stream_key, 6), dim), (blocks,), jnp.float32, smallest / len(pieces), largest / len(pieces))
        gain = gain * jnp.repeat(jnp.exp(steps), extent[dim] // blocks).reshape((-1,) + (1,) * (len(extent) - 1 - dim))
    return gain


def noise(key, shape, scale, bound, pieces=(), kind=jnp.bfloat16):
    array = jax.random.normal(key, shape, jnp.float32) * scale
    if len(pieces) > 0:
        array = shard_levels(key, shape, pieces, -0.22, 0.18) * array
    return jnp.clip(array, min=-bound, max=bound).astype(kind)


def setup_inputs(seed: int = 0) -> dict:
    splits = jax.random.split(jax.random.key(seed), 5)
    embeddings = noise(splits[0], (NROWS, D), 1.0, 6.0, ((0, 128),), jnp.float32)
    centroids = noise(splits[1], (CENTS, D), 1.0, 6.0, ((0, 4),), jnp.float32)
    owners = draw_owners(jax.random.fold_in(splits[4], 71), 0)
    live_blocks = draw_live_blocks(jax.random.fold_in(splits[4], 71), 0)
    return {"embeddings": embeddings, "centroids": centroids, "owners": owners, "live_blocks": live_blocks}


SCALE = 50.0
EPSILON = 1e-06
HIGHEST = lax.Precision.HIGHEST

def unit_of(values):
    squares = lax.optimization_barrier(jnp.sum(values * values, axis=-1, keepdims=True))
    return (values * lax.rsqrt(squares + EPSILON)).astype(jnp.bfloat16)

def sweep(row_tiles, centres, scaling, with_score):

    def one_tile(running, rows_tile):
        logits = jnp.dot(rows_tile, centres.T, preferred_element_type=jnp.float32) * SCALE
        weights = jnp.exp(logits)
        if scaling is None:
            inverse = jnp.ones((rows_tile.shape[0],), jnp.float32)
        else:
            inverse = 1.0 / jnp.dot(weights, scaling, precision=HIGHEST)
        running = running + jnp.dot(inverse, weights, precision=HIGHEST)
        if with_score:
            expected = inverse * jnp.dot(weights * logits, scaling, precision=HIGHEST)
        else:
            expected = inverse
        return (running, expected)
    initial = jnp.zeros((centres.shape[0],), jnp.float32)
    column, per_row = lax.scan(one_tile, initial, row_tiles)
    return (column, per_row.reshape(-1))

def reference(embeddings, centroids, owners, live_blocks):
    unit_rows = unit_of(embeddings)
    unit_cents = unit_of(centroids)
    row_count = unit_rows.shape[0]
    tile_rows = math.gcd(row_count, 1024)
    row_tiles = unit_rows.reshape(row_count // tile_rows, tile_rows, D)
    share_ratio = float(row_count) / CENTS
    column, expected = sweep(row_tiles, unit_cents, None, False)
    scaling = share_ratio / column
    for rounds in range(ITERS):
        column, expected = sweep(row_tiles, unit_cents, scaling, rounds == ITERS - 1)
        if rounds < ITERS - 1:
            scaling = share_ratio / column
    balance = scaling * column / share_ratio
    score_low = expected.astype(jnp.bfloat16)
    devices = live_blocks.shape[0]
    positions = jnp.arange(BLK, dtype=jnp.int32)
    owner_grid = owners.reshape(devices, BLK)
    live_mask = positions[None, :] < live_blocks[:, None]
    earlier = (owner_grid[:, None, :] == owner_grid[:, :, None]) & live_mask[:, None, :] & (positions[None, None, :] < positions[None, :, None])
    target = owner_grid * SLOT + lax.optimization_barrier(jnp.sum(earlier.astype(jnp.int32), axis=2))
    matches = (target[:, None, :] == jnp.arange(N_ROWS * SLOT, dtype=jnp.int32)[None, :, None]) & live_mask[:, None, :]
    source = lax.optimization_barrier(jnp.sum(jnp.where(matches, positions[None, None, :], 0), axis=2)) + jnp.where(jnp.any(matches, axis=2), 0, BLK)
    source = source.astype(jnp.int32)
    row_blocks = unit_rows.reshape(devices, BLK, BLOCK_ROWS, D)
    padded = jnp.concatenate([row_blocks, jnp.zeros((devices, 1, BLOCK_ROWS, D), jnp.bfloat16)], axis=1)
    score_blocks = score_low.reshape(devices, BLK, BLOCK_ROWS)
    padded_score = jnp.concatenate([score_blocks, jnp.zeros((devices, 1, BLOCK_ROWS), jnp.bfloat16)], axis=1)
    shipped = jax.vmap(lambda span_rows, index_row: span_rows[index_row])(padded, source)
    shipped_score = jax.vmap(lambda span_rows, index_row: span_rows[index_row])(padded_score, source)
    shipped = shipped.reshape(N_ROWS, N_CENT, N_ROWS, SLOT, BLOCK_ROWS, D).transpose(2, 1, 0, 3, 4, 5)
    shipped_score = shipped_score.reshape(N_ROWS, N_CENT, N_ROWS, SLOT, BLOCK_ROWS).transpose(2, 1, 0, 3, 4)
    moved = shipped.reshape(-1, D)
    moved_score = shipped_score.reshape(-1)
    return (moved, moved_score, balance)
```

```python
import functools
import math

import jax
import jax.numpy as jnp
from jax import lax
from jax.experimental import pallas as pl
from jax.experimental.pallas import tpu as pltpu
from jax.sharding import PartitionSpec as P

BLOCK_ROWS = 128
SCALE = 50.0
EPSILON = 1e-06
LOG2E = math.log2(math.e)
NT = (((1,), (1,)), ((), ()))
NN = (((1,), (0,)), ((), ()))
F32, BF16 = jnp.float32, jnp.bfloat16
NX, NY, NZ, NK = 4, 4, 4, 2
TILE = 512
MIB = 2**20


def params(mib):
    return pltpu.CompilerParams(vmem_limit_bytes=mib * MIB)


def x_perm(shift):
    return [(i, (i + shift) % NX) for i in range(NX)]


def rows_perm(dz, dy, dk):
    out = []
    for z in range(NZ):
        for y in range(NY):
            for k in range(NK):
                target = ((z + dz) % NZ * NY + (y + dy) % NY) * NK + (k + dk) % NK
                out.append(((z * NY + y) * NK + k, target))
    return out


def unit_f32(values):
    squares = jnp.sum(values * values, axis=-1, keepdims=True)
    return values * lax.rsqrt(squares + EPSILON)


def cents_kernel(place_ref, c_ref, all_ref, half_ref):
    step = pl.program_id(0)
    unit = unit_f32(c_ref[...]).astype(BF16)
    all_ref[...] = unit

    @pl.when(step == place_ref[0])
    def _():
        half_ref[...] = unit


def unit_cents(place, centroids):
    n, d = centroids.shape
    half = n // NK
    return pl.pallas_call(
        cents_kernel,
        grid_spec=pltpu.PrefetchScalarGridSpec(
            num_scalar_prefetch=1,
            grid=(NK,),
            in_specs=[pl.BlockSpec((half, d), lambda i, p: (i, 0))],
            out_specs=[
                pl.BlockSpec((half, d), lambda i, p: (i, 0)),
                pl.BlockSpec((half, d), lambda i, p: (0, 0)),
            ],
        ),
        out_shape=[jax.ShapeDtypeStruct((n, d), BF16), jax.ShapeDtypeStruct((half, d), BF16)],
        compiler_params=params(16),
        name="unit_cents",
    )(place, centroids)


def rows_kernel(owner_ref, live_ref, e_ref, out_ref, scaled_ref):
    step = pl.program_id(0)

    @pl.when(step == 0)
    def _():
        out_ref[...] = jnp.zeros_like(out_ref)

    unit = unit_f32(e_ref[...])
    scaled_ref[...] = (unit * (SCALE * LOG2E)).astype(BF16)
    low = unit.astype(BF16)
    count = e_ref.shape[0] // BLOCK_ROWS
    for b in range(count):
        block = step * count + b

        @pl.when(block < live_ref[0])
        def _():
            out_ref[owner_ref[block]] = low[b * BLOCK_ROWS : (b + 1) * BLOCK_ROWS]


def unit_rows(owners, live, embeddings, peers):
    n, d = embeddings.shape
    steps = 4
    return pl.pallas_call(
        rows_kernel,
        grid_spec=pltpu.PrefetchScalarGridSpec(
            num_scalar_prefetch=2,
            grid=(steps,),
            in_specs=[pl.BlockSpec((n // steps, d), lambda i, o, l: (i, 0))],
            out_specs=[
                pl.BlockSpec((peers, BLOCK_ROWS, d), lambda i, o, l: (0, 0, 0)),
                pl.BlockSpec((n // steps, d), lambda i, o, l: (i, 0)),
            ],
        ),
        out_shape=[
            jax.ShapeDtypeStruct((peers, BLOCK_ROWS, d), BF16),
            jax.ShapeDtypeStruct((n, d), BF16),
        ],
        compiler_params=params(24),
        name="unit_rows",
    )(owners, live, embeddings)


def column_sums(r_ref, c_ref, tr):
    n = c_ref.shape[0]
    tc = min(TILE, n)
    out = []
    for c in range(0, n, tc):
        cents = c_ref[c : c + tc, :]
        total = jnp.zeros((8, tc), F32)
        for i in range(0, r_ref.shape[0], tr):
            p = lax.dot_general(r_ref[i : i + tr, :], cents, NT, preferred_element_type=F32)
            total = total + jnp.exp2(p).reshape(tr // 8, 8, tc).sum(0)
        out.append(jnp.sum(total, axis=0, keepdims=True))
    return out


def first_kernel(r_ref, *refs):
    count = len(refs) // 2
    for c_ref, o_ref in zip(refs[:count], refs[count:]):
        tc = min(TILE, c_ref.shape[0])
        for j, part in enumerate(column_sums(r_ref, c_ref, 256)):
            o_ref[:, j * tc : (j + 1) * tc] = part


def first_sweep(scaled, pieces):
    return pl.pallas_call(
        first_kernel,
        out_shape=[jax.ShapeDtypeStruct((1, p.shape[0]), F32) for p in pieces],
        compiler_params=params(24),
        name="first_sweep",
    )(scaled, *pieces)


def last_kernel(off_ref, r_ref, *refs, n_new):
    pieces, ready, o_ref = refs[:n_new], refs[n_new:-1], refs[-1]
    tile = 0
    for ref in ready:
        for j in range(0, ref.shape[1], TILE):
            o_ref[:, pl.ds(pl.multiple_of(off_ref[tile], TILE), TILE)] = ref[:, j : j + TILE]
            tile += 1
    for c_ref in pieces:
        for part in column_sums(r_ref, c_ref, 256):
            o_ref[:, pl.ds(pl.multiple_of(off_ref[tile], TILE), TILE)] = part
            tile += 1


def last_sweep(offsets, scaled, pieces, ready):
    total = sum(p.shape[0] for p in pieces) + sum(p.shape[1] for p in ready)
    vmem = pl.BlockSpec(memory_space=pltpu.VMEM)
    return pl.pallas_call(
        functools.partial(last_kernel, n_new=len(pieces)),
        in_specs=[pl.BlockSpec(memory_space=pltpu.SMEM)] + [vmem] * (1 + len(pieces) + len(ready)),
        out_specs=vmem,
        out_shape=jax.ShapeDtypeStruct((1, total), F32),
        compiler_params=params(24),
        name="last_sweep",
    )(offsets, scaled, *pieces, *ready)


def lane_sum(x):
    parts = [x[:, j : j + 128] for j in range(0, x.shape[1], 128)]
    while len(parts) > 1:
        parts = [parts[i] + parts[i + 1] for i in range(0, len(parts), 2)]
    return parts[0]


def second_kernel(off_ref, r_ref, b_ref, *refs, n_pieces, tr, rg):
    pieces = refs[:n_pieces]
    col_ref, score_ref, e_scr, s_scr, u_scr, i_scr = refs[n_pieces:]
    rows = r_ref.shape[0]
    tiles = [(ref, j) for ref in pieces for j in range(0, ref.shape[0], TILE)]
    offsets = [pl.multiple_of(off_ref[i], TILE) for i in range(len(tiles))]
    col_ref[...] = jnp.zeros_like(col_ref)

    def body(t, carry):
        r = r_ref[pl.ds(pl.multiple_of(t * tr, tr), tr), :]
        for i, (ref, j) in enumerate(tiles):
            p = lax.dot_general(r, ref[j : j + TILE, :], NT, preferred_element_type=F32)
            bias = b_ref[:, pl.ds(offsets[i], TILE)]
            for g in range(0, tr, rg):
                part = p[g : g + rg]
                e = jnp.exp2(part + bias)
                e_scr[g : g + rg, i * TILE : (i + 1) * TILE] = e.astype(BF16)
                q = e * part
                if i == 0:
                    s_scr[g : g + rg] = lane_sum(e)
                    u_scr[g : g + rg] = lane_sum(q)
                else:
                    s_scr[g : g + rg] += lane_sum(e)
                    u_scr[g : g + rg] += lane_sum(q)
        inverse = 1.0 / jnp.sum(s_scr[...].T, axis=0, keepdims=True)
        weighted = jnp.sum(u_scr[...].T, axis=0, keepdims=True)
        score_ref[pl.ds(t, 1), :] = weighted * inverse * (1.0 / LOG2E)
        high = inverse.astype(BF16)
        low = (inverse - high.astype(F32)).astype(BF16)
        i_scr[...] = jnp.concatenate([high, low, jnp.zeros((14, tr), BF16)], axis=0)
        for i in range(len(tiles)):
            part = lax.dot_general(
                i_scr[...], e_scr[:, i * TILE : (i + 1) * TILE], NN, preferred_element_type=F32
            )
            col_ref[:, pl.ds(offsets[i], TILE)] += part[0:8]
        return carry

    lax.fori_loop(0, rows // tr, body, 0)


def second_sweep(offsets, scaled, bias, pieces):
    rows = scaled.shape[0]
    total = sum(p.shape[0] for p in pieces)
    tr = 256
    vmem = pl.BlockSpec(memory_space=pltpu.VMEM)
    return pl.pallas_call(
        functools.partial(second_kernel, n_pieces=len(pieces), tr=tr, rg=16),
        in_specs=[pl.BlockSpec(memory_space=pltpu.SMEM)] + [vmem] * (2 + len(pieces)),
        out_specs=[vmem, vmem],
        out_shape=[
            jax.ShapeDtypeStruct((8, total), F32),
            jax.ShapeDtypeStruct((rows // tr, tr), F32),
        ],
        scratch_shapes=[
            pltpu.VMEM((tr, total), BF16),
            pltpu.VMEM((tr, 128), F32),
            pltpu.VMEM((tr, 128), F32),
            pltpu.VMEM((16, tr), BF16),
        ],
        compiler_params=params(32),
        name="second_sweep",
    )(offsets, scaled, bias, *pieces)


def all_sum(values):
    for name, perms in (
        ("cent", [x_perm(s) for s in (1, 2, 3)]),
        ("rows", [rows_perm(0, s, 0) for s in (1, 2, 3)]),
        ("rows", [rows_perm(s, 0, 0) for s in (1, 2, 3)]),
        ("rows", [rows_perm(0, 0, 1)]),
    ):
        arrived = [lax.ppermute(values, name, perm) for perm in perms]
        for part in arrived:
            values = values + part
    return values


def local(embeddings, centroids, owners, live_blocks):
    x = lax.axis_index("cent")
    row_place = lax.axis_index("rows")
    k = row_place % NK
    y = row_place // NK % NY
    z = row_place // (NK * NY)
    n_cent, d = centroids.shape
    half = n_cent // NK
    rows = embeddings.shape[0]
    peers = NZ * NY * NK
    total = n_cent * NX

    own, mine = unit_cents(k.reshape(1).astype(jnp.int32), centroids)
    right = lax.ppermute(mine, "cent", x_perm(1))
    left = lax.ppermute(mine, "cent", x_perm(-1))
    outgoing, scaled = unit_rows(owners, live_blocks, embeddings, peers)
    arrived = lax.all_to_all(outgoing, "rows", split_axis=0, concat_axis=0, tiled=True)
    far_0 = lax.ppermute(right[: half // 2], "cent", x_perm(1))
    far_1 = lax.ppermute(left[half // 2 :], "cent", x_perm(-1))
    swap = rows_perm(0, 0, 1)
    right_o = lax.ppermute(right, "rows", swap)
    left_o = lax.ppermute(left, "rows", swap)
    far_0o = lax.ppermute(far_0, "rows", swap)
    far_1o = lax.ppermute(far_1, "rows", swap)

    def place(dx, kk, quarter):
        return (x + dx) % NX * n_cent + kk * half + quarter * TILE

    starts = [place(0, q // 2, q % 2) for q in range(4)]
    starts += [place(-1, k, 0), place(-1, k, 1), place(-1, 1 - k, 0), place(-1, 1 - k, 1)]
    starts += [place(1, k, 0), place(1, k, 1), place(1, 1 - k, 0), place(1, 1 - k, 1)]
    starts += [place(2, k, 0), place(2, k, 1), place(2, 1 - k, 0), place(2, 1 - k, 1)]
    offsets = jnp.stack(starts).astype(jnp.int32)

    sums_own = first_sweep(scaled, [own])
    sums_right = first_sweep(scaled, [right, right_o])
    sums_left = first_sweep(scaled, [left, left_o])
    far = [far_0, far_1, far_0o, far_1o]
    column = last_sweep(offsets, scaled, far, [*sums_own, *sums_right, *sums_left])
    column = all_sum(column)
    ratio = float(rows * NX * peers) / total
    bias = jnp.log2(ratio / column)
    pieces = [own, right, right_o, left, left_o, *far]
    column, score = second_sweep(offsets, scaled, bias, pieces)
    column = jnp.sum(column, axis=0)

    blocks = owners.shape[0]
    score = score.astype(BF16).astype(F32).reshape(blocks, BLOCK_ROWS)
    owner_z = (owners // (NK * NY) - z) % NZ
    owner_y = (owners // NK % NY - y) % NY
    owner_k = (owners % NK - k) % NK
    relative = (owner_z * NY + owner_y) * NK + owner_k
    live = jnp.arange(blocks, dtype=jnp.int32) < live_blocks[0]
    hit = (relative[None, :] == jnp.arange(peers, dtype=jnp.int32)[:, None]) & live[None, :]
    sent = jnp.sum(jnp.where(hit[:, :, None], score[None], 0.0), axis=1)
    sent = sent.reshape(NZ, NY * NK * BLOCK_ROWS)

    arrived_x = [lax.ppermute(column, "cent", x_perm(s)) for s in (1, 2, 3)]
    for part in arrived_x:
        column = column + part
    got = [sent[0]]
    new = column
    for s in (1, 2, 3):
        both = lax.ppermute(jnp.concatenate([column, sent[s]]), "rows", rows_perm(s, 0, 0))
        new = new + both[:total]
        got.append(both[total:])
    column = new
    sent = jnp.stack(got).reshape(NZ, NY, NK * BLOCK_ROWS)
    got = [sent[:, 0]]
    for s in (1, 2, 3):
        both = lax.ppermute(
            jnp.concatenate([column, sent[:, s].reshape(-1)]), "rows", rows_perm(0, s, 0)
        )
        new = new + both[:total]
        got.append(both[total:].reshape(NZ, NK * BLOCK_ROWS))
    column = new
    sent = jnp.stack(got, axis=1).reshape(NZ, NY, NK, BLOCK_ROWS)
    both = lax.ppermute(
        jnp.concatenate([column, sent[:, :, 1].reshape(-1)]), "rows", rows_perm(0, 0, 1)
    )
    column = column + both[:total]
    got = jnp.stack([sent[:, :, 0], both[total:].reshape(NZ, NY, BLOCK_ROWS)], axis=2)
    ids = jnp.arange(peers, dtype=jnp.int32)
    src = ((z - ids // (NK * NY)) % NZ * NY + (y - ids // NK % NY) % NY) * NK + (k - ids % NK) % NK
    hit = src[None, :] == ids[:, None]
    got = got.reshape(peers, BLOCK_ROWS)
    moved_score = jnp.sum(jnp.where(hit[:, :, None], got[None], 0.0), axis=1).astype(BF16)

    balance = column * (1.0 / ratio)
    return arrived.reshape(peers * BLOCK_ROWS, d), moved_score.reshape(-1), balance


def solution(mesh):
    placed = (P(("rows", "cent"), None), P("cent", None), P(("rows", "cent")), P(("rows", "cent")))
    return jax.shard_map(
        local,
        mesh=mesh,
        in_specs=placed,
        out_specs=(P(("rows", "cent"), None), P(("rows", "cent")), P()),
        check_vma=False,
    )
```

```python
import functools
import math

import jax
import jax.numpy as jnp
from jax import lax
from jax.experimental import pallas as pl
from jax.experimental.pallas import tpu as pltpu
from jax.sharding import PartitionSpec as P

BLOCK_ROWS = 128
SCALE = 50.0
EPSILON = 1e-06
LOG2E = math.log2(math.e)
NT = (((1,), (1,)), ((), ()))
NN = (((1,), (0,)), ((), ()))
F32, BF16 = jnp.float32, jnp.bfloat16
NX, NY, NZ, NK = 4, 4, 4, 2
TILE = 512
ROW_TILE = 512
MIB = 2**20


def params(mib):
    return pltpu.CompilerParams(vmem_limit_bytes=mib * MIB)


def in_hbm(x):
    return pltpu.with_memory_space_constraint(x, pltpu.HBM)


def in_vmem(x):
    return pltpu.with_memory_space_constraint(x, pltpu.VMEM)


def cost(rows, cents, passes):
    return pl.CostEstimate(flops=passes * rows, transcendentals=0, bytes_accessed=cents)


def x_perm(shift):
    return [(i, (i + shift) % NX) for i in range(NX)]


def rows_perm(dz, dy, dk):
    out = []
    for z in range(NZ):
        for y in range(NY):
            for k in range(NK):
                target = ((z + dz) % NZ * NY + (y + dy) % NY) * NK + (k + dk) % NK
                out.append(((z * NY + y) * NK + k, target))
    return out


def unit_f32(values):
    squares = jnp.sum(values * values, axis=-1, keepdims=True)
    return values * lax.rsqrt(squares + EPSILON)


def cents_kernel(place_ref, c_ref, all_ref, half_ref, buf, sems):
    half = buf.shape[1]
    copies = []
    for i in range(NK):
        start = pl.multiple_of((place_ref[0] ^ i) * half, half)
        copies.append(pltpu.make_async_copy(c_ref.at[pl.ds(start, half), :], buf.at[i], sems.at[i]))
    for copy in copies:
        copy.start()
    for i, copy in enumerate(copies):
        copy.wait()
        unit = unit_f32(buf[i]).astype(BF16)
        all_ref[pl.ds(pl.multiple_of((place_ref[0] ^ i) * half, half), half), :] = unit
        if i == 0:
            half_ref[...] = unit


def unit_cents(place, centroids):
    n, d = centroids.shape
    half = n // NK
    vmem = pl.BlockSpec(memory_space=pltpu.VMEM)
    return pl.pallas_call(
        cents_kernel,
        in_specs=[pl.BlockSpec(memory_space=pltpu.SMEM), pl.BlockSpec(memory_space=pltpu.HBM)],
        out_specs=[vmem, vmem],
        out_shape=[pltpu.VMEM((n, d), BF16), pltpu.VMEM((half, d), BF16)],
        scratch_shapes=[pltpu.VMEM((NK, half, d), F32), pltpu.SemaphoreType.DMA((NK,))],
        compiler_params=params(8),
        name="unit_cents",
    )(place, in_hbm(centroids))


def forward_kernel(right_ref, left_ref, first_ref, second_ref):
    n = first_ref.shape[0]
    first_ref[...] = right_ref[:n, :]
    second_ref[...] = left_ref[n:, :]


def forward_parts(right, left):
    n, d = right.shape
    vmem = pl.BlockSpec(memory_space=pltpu.VMEM)
    return pl.pallas_call(
        forward_kernel,
        in_specs=[vmem, vmem],
        out_specs=[vmem, vmem],
        out_shape=[jax.ShapeDtypeStruct((n // 2, d), BF16)] * 2,
        compiler_params=params(8),
        cost_estimate=cost(2**26, 0, 2**11),
        name="forward_parts",
    )(right, left)


def rows_kernel(owner_ref, live_ref, e_ref, out_ref, scaled_ref):
    step = pl.program_id(0)

    @pl.when(step == 0)
    def _():
        out_ref[...] = jnp.zeros_like(out_ref)

    unit = unit_f32(e_ref[...])
    scaled_ref[...] = (unit * (SCALE * LOG2E)).astype(BF16)
    low = unit.astype(BF16)
    count = e_ref.shape[0] // BLOCK_ROWS
    for b in range(count):
        block = step * count + b

        @pl.when(block < live_ref[0])
        def _():
            out_ref[owner_ref[block]] = low[b * BLOCK_ROWS : (b + 1) * BLOCK_ROWS]


def unit_rows(owners, live, embeddings, peers):
    n, d = embeddings.shape
    steps = 4
    return pl.pallas_call(
        rows_kernel,
        grid_spec=pltpu.PrefetchScalarGridSpec(
            num_scalar_prefetch=2,
            grid=(steps,),
            in_specs=[pl.BlockSpec((n // steps, d), lambda i, o, l: (i, 0))],
            out_specs=[
                pl.BlockSpec((peers, BLOCK_ROWS, d), lambda i, o, l: (0, 0, 0)),
                pl.BlockSpec((n // steps, d), lambda i, o, l: (i, 0)),
            ],
        ),
        out_shape=[pltpu.HBM((peers, BLOCK_ROWS, d), BF16), pltpu.VMEM((n, d), BF16)],
        compiler_params=params(8),
        name="unit_rows",
    )(owners, live, embeddings)


def column_sums(r_ref, c_ref, tr):
    n = c_ref.shape[0]
    tc = min(TILE, n)
    out = []
    for c in range(0, n, tc):
        cents = c_ref[c : c + tc, :]
        total = jnp.zeros((8, tc), F32)
        for i in range(0, r_ref.shape[0], tr):
            p = lax.dot_general(r_ref[i : i + tr, :], cents, NT, preferred_element_type=F32)
            total = total + jnp.exp2(p).reshape(tr // 8, 8, tc).sum(0)
        out.append(jnp.sum(total, axis=0, keepdims=True))
    return out


def first_kernel(r_ref, *refs):
    count = len(refs) // 2
    for c_ref, o_ref in zip(refs[:count], refs[count:]):
        tc = min(TILE, c_ref.shape[0])
        for j, part in enumerate(column_sums(r_ref, c_ref, 256)):
            o_ref[:, j * tc : (j + 1) * tc] = part


def first_sweep(scaled, pieces):
    return pl.pallas_call(
        first_kernel,
        out_shape=[pltpu.VMEM((1, p.shape[0]), F32) for p in pieces],
        compiler_params=params(8),
        cost_estimate=cost(scaled.shape[0], sum(p.shape[0] for p in pieces), 1),
        name="first_sweep",
    )(in_vmem(scaled), *[in_vmem(p) for p in pieces])


def last_kernel(off_ref, r_ref, *refs, n_new):
    pieces, ready, o_ref = refs[:n_new], refs[n_new:-1], refs[-1]
    parts = [ref[:, j : j + TILE] for ref in ready for j in range(0, ref.shape[1], TILE)]
    for c_ref in pieces:
        parts += column_sums(r_ref, c_ref, 256)
    for tile, part in enumerate(parts):
        for j in range(TILE // 128):
            o_ref[pl.ds(off_ref[tile] + j, 1), :] = part[:, j * 128 : (j + 1) * 128]


def last_sweep(offsets, scaled, pieces, ready):
    total = sum(p.shape[0] for p in pieces) + sum(p.shape[1] for p in ready)
    vmem = pl.BlockSpec(memory_space=pltpu.VMEM)
    return pl.pallas_call(
        functools.partial(last_kernel, n_new=len(pieces)),
        in_specs=[pl.BlockSpec(memory_space=pltpu.SMEM)] + [vmem] * (1 + len(pieces) + len(ready)),
        out_specs=vmem,
        out_shape=jax.ShapeDtypeStruct((total // 128, 128), F32),
        compiler_params=params(8),
        cost_estimate=cost(scaled.shape[0], sum(p.shape[0] for p in pieces), 1),
        name="last_sweep",
    )(offsets, *[in_vmem(p) for p in (scaled, *pieces, *ready)])


def lane_sum(x):
    parts = [x[:, j : j + 128] for j in range(0, x.shape[1], 128)]
    while len(parts) > 1:
        parts = [parts[i] + parts[i + 1] for i in range(0, len(parts), 2)]
    return parts[0]


def second_kernel(off_ref, r_ref, first_ref, in_ref, *refs, n_pieces, tr, rg, ratio):
    pieces = refs[:n_pieces]
    out_ref, score_ref, moved_ref, *scratch = refs[n_pieces:]
    b_scr, col_scr, e_scr, s_scr, u_scr, i_scr, c_scr, m_scr, sem, sems = scratch
    rows = r_ref.shape[0]
    copies = []
    at = 0
    for i, ref in enumerate(pieces):
        n = ref.shape[0]
        copies.append(pltpu.make_async_copy(ref, c_scr.at[at : at + n, :], sems.at[i]))
        copies[-1].start()
        at += n
    load = pltpu.make_async_copy(in_ref, m_scr, sem.at[0])
    load.start()
    store = pltpu.make_async_copy(m_scr, moved_ref, sem.at[1])
    tiles = range(0, c_scr.shape[0], TILE)
    n_own = pieces[0].shape[0] // TILE
    lanes = TILE // 128
    for i in range(len(tiles)):
        for j in range(lanes):
            at = (i * lanes + j) * 128
            b_scr[:, at : at + 128] = first_ref[pl.ds(off_ref[i] + j, 1), :]
    b_scr[...] = jnp.log2(ratio / b_scr[...])
    copies[0].wait()
    col_scr[...] = jnp.zeros_like(col_scr)
    width = 256

    def body(t, carry):
        r = r_ref[pl.ds(pl.multiple_of(t * tr, tr), tr), :]
        for i, j in enumerate(tiles):
            if i == n_own:

                @pl.when(t == 0)
                def _():
                    for piece in copies[1:]:
                        piece.wait()
                    load.wait()
                    store.start()

            here = slice(i * TILE, (i + 1) * TILE)
            p = lax.dot_general(r, c_scr[j : j + TILE, :], NT, preferred_element_type=F32)
            bias = b_scr[:, here]
            for g in range(0, tr, rg):
                part = p[g : g + rg]
                e = jnp.exp2(part + bias)
                e_scr[g : g + rg, here] = e.astype(BF16)
                q = e * part
                if i == 0:
                    s_scr[g : g + rg] = lane_sum(e)
                    u_scr[g : g + rg] = lane_sum(q)
                else:
                    s_scr[g : g + rg] += lane_sum(e)
                    u_scr[g : g + rg] += lane_sum(q)
        for g in range(0, tr, width):
            inverse = 1.0 / jnp.sum(s_scr[g : g + width].T, axis=0, keepdims=True)
            weighted = jnp.sum(u_scr[g : g + width].T, axis=0, keepdims=True)
            place = t * (tr // width) + g // width
            score_ref[pl.ds(place, 1), :] = weighted * inverse * (1.0 / LOG2E)
            high = inverse.astype(BF16)
            low = (inverse - high.astype(F32)).astype(BF16)
            i_scr[:, g : g + width] = jnp.concatenate(
                [high, low, jnp.zeros((14, width), BF16)], axis=0
            )
        for i in range(len(tiles)):
            here = slice(i * TILE, (i + 1) * TILE)
            part = lax.dot_general(i_scr[...], e_scr[:, here], NN, preferred_element_type=F32)
            col_scr[:, here] += part[0:8]
        return carry

    lax.fori_loop(0, rows // tr, body, 0)
    for i in range(len(tiles)):
        for j in range(lanes):
            at = (i * lanes + j) * 128
            line = jnp.sum(col_scr[:, at : at + 128], axis=0, keepdims=True)
            out_ref[pl.ds(off_ref[i] + j, 1), :] = line
    store.wait()


def second_sweep(offsets, scaled, first, arrived, pieces, ratio):
    rows = scaled.shape[0]
    total = sum(p.shape[0] for p in pieces)
    tr = ROW_TILE
    vmem = pl.BlockSpec(memory_space=pltpu.VMEM)
    any_space = pl.BlockSpec(memory_space=pl.ANY)
    return pl.pallas_call(
        functools.partial(second_kernel, n_pieces=len(pieces), tr=tr, rg=16, ratio=ratio),
        in_specs=[pl.BlockSpec(memory_space=pltpu.SMEM), vmem, vmem, any_space]
        + [any_space] * len(pieces),
        out_specs=[vmem, vmem, any_space],
        out_shape=[
            jax.ShapeDtypeStruct((total // 128, 128), F32),
            jax.ShapeDtypeStruct((rows // 256, 256), F32),
            pltpu.HBM(arrived.shape, BF16),
        ],
        scratch_shapes=[
            pltpu.VMEM((1, total), F32),
            pltpu.VMEM((8, total), F32),
            pltpu.VMEM((tr, total), BF16),
            pltpu.VMEM((tr, 128), F32),
            pltpu.VMEM((tr, 128), F32),
            pltpu.VMEM((16, tr), BF16),
            pltpu.VMEM((total, scaled.shape[1]), BF16),
            pltpu.VMEM(arrived.shape, BF16),
            pltpu.SemaphoreType.DMA((2,)),
            pltpu.SemaphoreType.DMA((len(pieces),)),
        ],
        compiler_params=params(26),
        cost_estimate=cost(rows, total, 3),
        name="second_sweep",
    )(offsets, in_vmem(scaled), first, in_hbm(arrived), *pieces)


def finish_kernel(place_ref, col_ref, last_ref, kept_ref, bal_ref, out_ref, buf, *, scale):
    lines = col_ref.shape[0]
    bal_ref[...] = (col_ref[...] + last_ref[:lines, :]) * scale
    z, y, k = place_ref[0], place_ref[1], place_ref[2]
    for dz in range(NZ):
        for dy in range(NY):
            at = dz * NY + dy
            to = (((z - dz) & (NZ - 1)) * NY + ((y - dy) & (NY - 1))) * NK
            buf[pl.ds(to + k, 1), :] = kept_ref[at : at + 1, :]
            buf[pl.ds(to + 1 - k, 1), :] = last_ref[lines + at : lines + at + 1, :]
    out_ref[...] = buf[...].astype(BF16)


def finish(place, column, last, kept, scale):
    peers = NZ * NY * NK
    vmem = pl.BlockSpec(memory_space=pltpu.VMEM)
    return pl.pallas_call(
        functools.partial(finish_kernel, scale=scale),
        in_specs=[pl.BlockSpec(memory_space=pltpu.SMEM), vmem, vmem, vmem],
        out_specs=[vmem, vmem],
        out_shape=[
            jax.ShapeDtypeStruct(column.shape, F32),
            jax.ShapeDtypeStruct((peers, 128), BF16),
        ],
        scratch_shapes=[pltpu.VMEM((peers, 128), F32)],
        compiler_params=params(8),
        name="finish",
    )(place, column, last, kept)


def all_sum(values, other):
    for name, perms in (
        ("cent", [x_perm(s) for s in (1, 3, 2)]),
        ("rows", [rows_perm(0, 0, 1)]),
        ("rows", [rows_perm(0, s, 0) for s in (1, 3, 2)]),
        ("rows", [rows_perm(s, 0, 0) for s in (1, 3, 2)]),
    ):
        arrived = [lax.ppermute(values, name, perm) for perm in perms]
        for part in arrived:
            values = values + part
    values, other = lax.optimization_barrier((values, other))
    return values, other


def local(embeddings, centroids, owners, live_blocks):
    x = lax.axis_index("cent")
    row_place = lax.axis_index("rows")
    k = row_place & (NK - 1)
    y = (row_place // NK) & (NY - 1)
    z = row_place // (NK * NY)
    n_cent, d = centroids.shape
    half = n_cent // NK
    rows = embeddings.shape[0]
    peers = NZ * NY * NK
    total = n_cent * NX

    place = jnp.stack([z, y, k]).astype(jnp.int32)
    own, mine = unit_cents(k.reshape(1).astype(jnp.int32), centroids)
    right = lax.ppermute(mine, "cent", x_perm(1))
    left = lax.ppermute(mine, "cent", x_perm(-1))
    embeddings, mine = lax.optimization_barrier((embeddings, mine))
    outgoing, scaled = unit_rows(owners, live_blocks, embeddings, peers)
    arrived = lax.all_to_all(outgoing, "rows", split_axis=0, concat_axis=0, tiled=True)
    right, left, scaled = lax.optimization_barrier((right, left, scaled))
    swap = rows_perm(0, 0, 1)
    far = [lax.ppermute(t, "cent", x_perm(s)) for t, s in zip(forward_parts(right, left), (1, -1))]
    right = [right, lax.ppermute(right, "rows", swap)]
    left = [left, lax.ppermute(left, "rows", swap)]
    sums_own = first_sweep(scaled, [own])
    sums_right = first_sweep(scaled, right)
    sums_left = first_sweep(scaled, left)
    far, sums_own, sums_right, sums_left = lax.optimization_barrier(
        (far, sums_own, sums_right, sums_left)
    )
    far += [lax.ppermute(t, "rows", swap) for t in far]

    def line(dx, kk, quarter):
        return (((x + dx) & (NX - 1)) * n_cent + kk * half + quarter * TILE) // 128

    starts = [line(0, q // 2, q % 2) for q in range(4)]
    for dx in (-1, 1, 2):
        starts += [line(dx, k, 0), line(dx, k, 1), line(dx, 1 - k, 0), line(dx, 1 - k, 1)]
    offsets = jnp.stack(starts).astype(jnp.int32)

    column = last_sweep(offsets, scaled, far, [*sums_own, *sums_right, *sums_left])
    column, arrived = all_sum(column, arrived)
    ratio = float(rows * NX * peers) / total
    pieces = [own, right[0], in_hbm(right[1]), left[0], in_hbm(left[1]), *far]
    column, score, moved = second_sweep(offsets, scaled, column, arrived, pieces, ratio)

    blocks = owners.shape[0]
    score = score.astype(BF16).astype(F32).reshape(blocks, BLOCK_ROWS)
    owner_z = (owners // (NK * NY) - z) & (NZ - 1)
    owner_y = (owners // NK - y) & (NY - 1)
    owner_k = (owners - k) & (NK - 1)
    relative = (owner_z * NY + owner_y) * NK + owner_k
    live = jnp.arange(blocks, dtype=jnp.int32) < live_blocks[0]
    hit = (relative[None, :] == jnp.arange(peers, dtype=jnp.int32)[:, None]) & live[None, :]
    sent = jnp.sum(jnp.where(hit[:, :, None], score[None], 0.0), axis=1)
    sent = sent.reshape(NZ, NY * NK, BLOCK_ROWS)
    lines = total // 128

    for part in [lax.ppermute(column, "cent", x_perm(s)) for s in (1, 3, 2)]:
        column = column + part
    both = [
        lax.ppermute(jnp.concatenate([column, sent[s]]), "rows", rows_perm(s, 0, 0))
        for s in (1, 3, 2)
    ]
    column = column + both[0][:lines] + both[1][:lines] + both[2][:lines]
    both = [both[0], both[2], both[1]]
    sent = jnp.stack([sent[0]] + [b[lines:] for b in both]).reshape(NZ, NY, NK, BLOCK_ROWS)
    both = [
        lax.ppermute(
            jnp.concatenate([column, sent[:, s].reshape(NZ * NK, BLOCK_ROWS)]),
            "rows",
            rows_perm(0, s, 0),
        )
        for s in (1, 3, 2)
    ]
    column = column + both[0][:lines] + both[1][:lines] + both[2][:lines]
    both = [both[0], both[2], both[1]]
    got = [b[lines:].reshape(NZ, NK, BLOCK_ROWS) for b in both]
    sent = jnp.stack([sent[:, 0], *got], axis=1)
    kept = sent[:, :, 0].reshape(NZ * NY, BLOCK_ROWS)
    given = sent[:, :, 1].reshape(NZ * NY, BLOCK_ROWS)
    last = lax.ppermute(jnp.concatenate([column, given]), "rows", swap)
    balance, moved_score = finish(place, column, last, kept, 1.0 / ratio)
    return moved.reshape(peers * BLOCK_ROWS, d), moved_score.reshape(-1), balance.reshape(-1)


def solution(mesh):
    placed = (P(("rows", "cent"), None), P("cent", None), P(("rows", "cent")), P(("rows", "cent")))
    return jax.shard_map(
        local,
        mesh=mesh,
        in_specs=placed,
        out_specs=(P(("rows", "cent"), None), P(("rows", "cent")), P()),
        check_vma=False,
    )
```

```python
import functools
import math

import jax
import jax.numpy as jnp
from jax import lax
from jax.experimental import pallas as pl
from jax.experimental.pallas import tpu as pltpu
from jax.sharding import PartitionSpec as P

BLOCK_ROWS = 128
SCALE = 50.0
EPSILON = 1e-06
LOG2E = math.log2(math.e)
NT = (((1,), (1,)), ((), ()))
NN = (((1,), (0,)), ((), ()))
F32, BF16 = jnp.float32, jnp.bfloat16
NX, NY, NZ, NK = 4, 4, 4, 2
TILE = 512
ROW_TILE = 512
MIB = 2**20


def params(mib):
    return pltpu.CompilerParams(vmem_limit_bytes=mib * MIB)


def in_hbm(x):
    return pltpu.with_memory_space_constraint(x, pltpu.HBM)


def in_vmem(x):
    return pltpu.with_memory_space_constraint(x, pltpu.VMEM)


def cost(rows, cents, passes):
    return pl.CostEstimate(flops=passes * rows, transcendentals=0, bytes_accessed=cents)


def x_perm(shift):
    return [(i, (i + shift) % NX) for i in range(NX)]


def rows_perm(dz, dy, dk):
    out = []
    for z in range(NZ):
        for y in range(NY):
            for k in range(NK):
                target = ((z + dz) % NZ * NY + (y + dy) % NY) * NK + (k + dk) % NK
                out.append(((z * NY + y) * NK + k, target))
    return out


def unit_f32(values):
    squares = jnp.sum(values * values, axis=-1, keepdims=True)
    return values * lax.rsqrt(squares + EPSILON)


def cents_kernel(place_ref, c_ref, all_ref, half_ref, buf, sems):
    half = buf.shape[1]
    copies = []
    for i in range(NK):
        start = pl.multiple_of((place_ref[0] ^ i) * half, half)
        copies.append(pltpu.make_async_copy(c_ref.at[pl.ds(start, half), :], buf.at[i], sems.at[i]))
    for copy in copies:
        copy.start()
    for i, copy in enumerate(copies):
        copy.wait()
        unit = unit_f32(buf[i]).astype(BF16)
        all_ref[pl.ds(pl.multiple_of((place_ref[0] ^ i) * half, half), half), :] = unit
        if i == 0:
            half_ref[...] = unit


def unit_cents(place, centroids):
    n, d = centroids.shape
    half = n // NK
    vmem = pl.BlockSpec(memory_space=pltpu.VMEM)
    return pl.pallas_call(
        cents_kernel,
        in_specs=[pl.BlockSpec(memory_space=pltpu.SMEM), pl.BlockSpec(memory_space=pltpu.HBM)],
        out_specs=[vmem, vmem],
        out_shape=[pltpu.VMEM((n, d), BF16), pltpu.VMEM((half, d), BF16)],
        scratch_shapes=[pltpu.VMEM((NK, half, d), F32), pltpu.SemaphoreType.DMA((NK,))],
        compiler_params=params(8),
        name="unit_cents",
    )(place, in_hbm(centroids))


def sum_kernel(in_ref, out_ref):
    total = in_ref[0]
    for i in range(1, in_ref.shape[0]):
        total = total + in_ref[i]
    out_ref[...] = total


def sum_blocks(blocks):
    return pl.pallas_call(
        sum_kernel,
        out_shape=pltpu.VMEM(blocks.shape[1:], F32),
        compiler_params=params(4),
        name="sum_blocks",
    )(in_vmem(blocks))


def forward_kernel(right_ref, left_ref, first_ref, second_ref):
    n = first_ref.shape[0]
    first_ref[...] = right_ref[:n, :]
    second_ref[...] = left_ref[n:, :]


def forward_parts(right, left):
    n, d = right.shape
    vmem = pl.BlockSpec(memory_space=pltpu.VMEM)
    return pl.pallas_call(
        forward_kernel,
        in_specs=[vmem, vmem],
        out_specs=[vmem, vmem],
        out_shape=[jax.ShapeDtypeStruct((n // 2, d), BF16)] * 2,
        compiler_params=params(8),
        cost_estimate=cost(2**26, 0, 2**11),
        name="forward_parts",
    )(right, left)


def rows_kernel(owner_ref, live_ref, e_ref, out_ref, scaled_ref):
    step = pl.program_id(0)

    @pl.when(step == 0)
    def _():
        out_ref[...] = jnp.zeros_like(out_ref)

    unit = unit_f32(e_ref[...])
    scaled_ref[...] = (unit * (SCALE * LOG2E)).astype(BF16)
    low = unit.astype(BF16)
    count = e_ref.shape[0] // BLOCK_ROWS
    for b in range(count):
        block = step * count + b

        @pl.when(block < live_ref[0])
        def _():
            out_ref[owner_ref[block]] = low[b * BLOCK_ROWS : (b + 1) * BLOCK_ROWS]


def unit_rows(owners, live, embeddings, peers):
    n, d = embeddings.shape
    steps = 4
    return pl.pallas_call(
        rows_kernel,
        grid_spec=pltpu.PrefetchScalarGridSpec(
            num_scalar_prefetch=2,
            grid=(steps,),
            in_specs=[pl.BlockSpec((n // steps, d), lambda i, o, l: (i, 0))],
            out_specs=[
                pl.BlockSpec((peers, BLOCK_ROWS, d), lambda i, o, l: (0, 0, 0)),
                pl.BlockSpec((n // steps, d), lambda i, o, l: (i, 0)),
            ],
        ),
        out_shape=[pltpu.HBM((peers, BLOCK_ROWS, d), BF16), pltpu.VMEM((n, d), BF16)],
        compiler_params=params(8),
        name="unit_rows",
    )(owners, live, embeddings)


def column_sums(r_ref, c_ref, tr):
    n = c_ref.shape[0]
    tc = min(TILE, n)
    out = []
    for c in range(0, n, tc):
        cents = c_ref[c : c + tc, :]
        total = jnp.zeros((8, tc), F32)
        for i in range(0, r_ref.shape[0], tr):
            p = lax.dot_general(r_ref[i : i + tr, :], cents, NT, preferred_element_type=F32)
            total = total + jnp.exp2(p).reshape(tr // 8, 8, tc).sum(0)
        out.append(jnp.sum(total, axis=0, keepdims=True))
    return out


def first_kernel(r_ref, *refs):
    count = len(refs) // 2
    for c_ref, o_ref in zip(refs[:count], refs[count:]):
        tc = min(TILE, c_ref.shape[0])
        for j, part in enumerate(column_sums(r_ref, c_ref, 256)):
            o_ref[:, j * tc : (j + 1) * tc] = part


def first_sweep(scaled, pieces):
    return pl.pallas_call(
        first_kernel,
        out_shape=[pltpu.VMEM((1, p.shape[0]), F32) for p in pieces],
        compiler_params=params(8),
        cost_estimate=cost(scaled.shape[0], sum(p.shape[0] for p in pieces), 1),
        name="first_sweep",
    )(in_vmem(scaled), *[in_vmem(p) for p in pieces])


def last_kernel(off_ref, r_ref, *refs, n_new):
    pieces, ready, (keep_ref, give_ref, buf) = refs[:n_new], refs[n_new:-3], refs[-3:]
    parts = [ref[:, j : j + TILE] for ref in ready for j in range(0, ref.shape[1], TILE)]
    for c_ref in pieces:
        parts += column_sums(r_ref, c_ref, 256)
    for tile, part in enumerate(parts):
        for j in range(TILE // 128):
            buf[pl.ds(off_ref[tile] + j, 1), :] = part[:, j * 128 : (j + 1) * 128]
    half = keep_ref.shape[0]
    keep_ref[...] = buf[:half, :]
    give_ref[...] = buf[half:, :]


def last_sweep(offsets, scaled, pieces, ready):
    total = sum(p.shape[0] for p in pieces) + sum(p.shape[1] for p in ready)
    vmem = pl.BlockSpec(memory_space=pltpu.VMEM)
    half = total // 128 // NK
    return pl.pallas_call(
        functools.partial(last_kernel, n_new=len(pieces)),
        in_specs=[pl.BlockSpec(memory_space=pltpu.SMEM)] + [vmem] * (1 + len(pieces) + len(ready)),
        out_specs=[vmem, vmem],
        out_shape=[pltpu.VMEM((half, 128), F32)] * 2,
        scratch_shapes=[pltpu.VMEM((NK * half, 128), F32)],
        compiler_params=params(8),
        cost_estimate=cost(scaled.shape[0], sum(p.shape[0] for p in pieces), 1),
        name="last_sweep",
    )(offsets, *[in_vmem(p) for p in (scaled, *pieces, *ready)])


def lane_sum(x):
    parts = [x[:, j : j + 128] for j in range(0, x.shape[1], 128)]
    while len(parts) > 1:
        parts = [parts[i] + parts[i + 1] for i in range(0, len(parts), 2)]
    return parts[0]


def second_kernel(
    off_ref, to_ref, live_ref, r_ref, mine_ref, other_ref, in_ref, *refs, n_pieces, tr, rg, ratio
):
    pieces = refs[:n_pieces]
    keep_ref, sent_ref, give_ref, moved_ref, *scratch = refs[n_pieces:]
    line_scr, score_scr, b_scr, col_scr, e_scr, s_scr, u_scr, i_scr, c_scr, m_scr, sem, sems = scratch
    rows = r_ref.shape[0]
    copies = []
    at = 0
    for i, ref in enumerate(pieces):
        n = ref.shape[0]
        copies.append(pltpu.make_async_copy(ref, c_scr.at[at : at + n, :], sems.at[i]))
        copies[-1].start()
        at += n
    load = pltpu.make_async_copy(in_ref, m_scr, sem.at[0])
    load.start()
    store = pltpu.make_async_copy(m_scr, moved_ref, sem.at[1])
    tiles = range(0, c_scr.shape[0], TILE)
    n_own = pieces[0].shape[0] // TILE
    lanes = TILE // 128
    half = mine_ref.shape[0]
    line_scr[:half, :] = jnp.log2(ratio / mine_ref[...])
    line_scr[half:, :] = jnp.log2(ratio / other_ref[...])
    for i in range(len(tiles)):
        for j in range(lanes):
            at = (i * lanes + j) * 128
            b_scr[:, at : at + 128] = line_scr[pl.ds(off_ref[i] + j, 1), :]
    copies[0].wait()
    col_scr[...] = jnp.zeros_like(col_scr)
    width = 256

    def body(t, carry):
        r = r_ref[pl.ds(pl.multiple_of(t * tr, tr), tr), :]
        for i, j in enumerate(tiles):
            if i == n_own:

                @pl.when(t == 0)
                def _():
                    for piece in copies[1:]:
                        piece.wait()
                    load.wait()
                    store.start()

            here = slice(i * TILE, (i + 1) * TILE)
            p = lax.dot_general(r, c_scr[j : j + TILE, :], NT, preferred_element_type=F32)
            bias = b_scr[:, here]
            for g in range(0, tr, rg):
                part = p[g : g + rg]
                e = jnp.exp2(part + bias)
                e_scr[g : g + rg, here] = e.astype(BF16)
                q = e * part
                if i == 0:
                    s_scr[g : g + rg] = lane_sum(e)
                    u_scr[g : g + rg] = lane_sum(q)
                else:
                    s_scr[g : g + rg] += lane_sum(e)
                    u_scr[g : g + rg] += lane_sum(q)
        for g in range(0, tr, width):
            inverse = 1.0 / jnp.sum(s_scr[g : g + width].T, axis=0, keepdims=True)
            weighted = jnp.sum(u_scr[g : g + width].T, axis=0, keepdims=True)
            place = t * (tr // width) + g // width
            score_scr[pl.ds(place, 1), :] = weighted * inverse * (1.0 / LOG2E)
            high = inverse.astype(BF16)
            low = (inverse - high.astype(F32)).astype(BF16)
            i_scr[:, g : g + width] = jnp.concatenate(
                [high, low, jnp.zeros((14, width), BF16)], axis=0
            )
        for i in range(len(tiles)):
            here = slice(i * TILE, (i + 1) * TILE)
            part = lax.dot_general(i_scr[...], e_scr[:, here], NN, preferred_element_type=F32)
            col_scr[:, here] += part[0:8]
        return carry

    lax.fori_loop(0, rows // tr, body, 0)
    for i in range(len(tiles)):
        for j in range(lanes):
            at = (i * lanes + j) * 128
            line = jnp.sum(col_scr[:, at : at + 128], axis=0, keepdims=True)
            line_scr[pl.ds(off_ref[i] + j, 1), :] = line
    keep_ref[...] = line_scr[:half, :]
    give_ref[:half, :] = line_scr[half:, :]
    blocks = rows // BLOCK_ROWS
    peers = NZ * NY
    line_scr[: NK * peers, :] = jnp.zeros((NK * peers, BLOCK_ROWS), F32)
    for b in range(blocks):
        at = b % 2 * BLOCK_ROWS

        @pl.when(b < live_ref[0])
        def _():
            score = score_scr[b // 2 : b // 2 + 1, at : at + BLOCK_ROWS]
            line_scr[pl.ds(to_ref[b], 1), :] = score.astype(BF16).astype(F32)

    sent_ref[...] = line_scr[:peers, :]
    give_ref[half:, :] = line_scr[peers : NK * peers, :]
    store.wait()


def second_sweep(offsets, targets, live, scaled, mine, other, arrived, pieces, ratio):
    rows = scaled.shape[0]
    total = sum(p.shape[0] for p in pieces)
    tr = ROW_TILE
    half = mine.shape[0]
    peers = NZ * NY
    vmem = pl.BlockSpec(memory_space=pltpu.VMEM)
    smem = pl.BlockSpec(memory_space=pltpu.SMEM)
    any_space = pl.BlockSpec(memory_space=pl.ANY)
    return pl.pallas_call(
        functools.partial(second_kernel, n_pieces=len(pieces), tr=tr, rg=16, ratio=ratio),
        in_specs=[smem, smem, smem, vmem, vmem, vmem, any_space] + [any_space] * len(pieces),
        out_specs=[vmem, vmem, vmem, any_space],
        out_shape=[
            pltpu.VMEM((half, 128), F32),
            pltpu.VMEM((peers, BLOCK_ROWS), F32),
            pltpu.VMEM((half + peers, 128), F32),
            pltpu.HBM(arrived.shape, BF16),
        ],
        scratch_shapes=[
            pltpu.VMEM((total // 128, 128), F32),
            pltpu.VMEM((rows // 256, 256), F32),
            pltpu.VMEM((1, total), F32),
            pltpu.VMEM((8, total), F32),
            pltpu.VMEM((tr, total), BF16),
            pltpu.VMEM((tr, 128), F32),
            pltpu.VMEM((tr, 128), F32),
            pltpu.VMEM((16, tr), BF16),
            pltpu.VMEM((total, scaled.shape[1]), BF16),
            pltpu.VMEM(arrived.shape, BF16),
            pltpu.SemaphoreType.DMA((2,)),
            pltpu.SemaphoreType.DMA((len(pieces),)),
        ],
        compiler_params=params(26),
        cost_estimate=cost(rows, total, 3),
        name="second_sweep",
    )(offsets, targets, live, in_vmem(scaled), mine, other, in_hbm(arrived), *pieces)


def pack_kernel(k_ref, col_ref, a_ref, b_ref, c_ref, sent_ref, got_ref, out_ref):
    half = col_ref.shape[0]
    peers = sent_ref.shape[0]
    out_ref[:, :half, :] = jnp.broadcast_to(
        (col_ref[...] + a_ref[...] + (b_ref[...] + c_ref[...]))[None], (peers, half, 128)
    )
    out_ref[:, half:, :] = jnp.zeros((peers, out_ref.shape[1] - half, 128), F32)
    k = k_ref[0]
    for i in range(peers):
        out_ref[i, pl.ds(half + k, 1), :] = sent_ref[i : i + 1, :]
        out_ref[i, pl.ds(half + 1 - k, 1), :] = got_ref[half + i : half + i + 1, :]


def pack(k, column, arrived, sent, got):
    half, peers = column.shape[0], sent.shape[0]
    vmem = pl.BlockSpec(memory_space=pltpu.VMEM)
    return pl.pallas_call(
        pack_kernel,
        in_specs=[pl.BlockSpec(memory_space=pltpu.SMEM)] + [vmem] * 6,
        out_specs=vmem,
        out_shape=jax.ShapeDtypeStruct((peers, half + 8, 128), F32),
        compiler_params=params(4),
        name="pack",
    )(k, column, *arrived, sent, got)


def finish_kernel(k_ref, mine_ref, other_ref, all_ref, bal_ref, out_ref, *, scale):
    half = mine_ref.shape[0]
    k = k_ref[0]
    bal_ref[pl.ds(pl.multiple_of(k * half, half), half), :] = mine_ref[...] * scale
    bal_ref[pl.ds(pl.multiple_of((1 - k) * half, half), half), :] = other_ref[...] * scale
    peers = all_ref.shape[0]
    scores = jnp.concatenate([all_ref[i, half : half + NK, :] for i in range(peers)], axis=0)
    out_ref[...] = scores.astype(BF16)


def finish(k, mine, other, everything, scale):
    half, peers = mine.shape[0], everything.shape[0]
    vmem = pl.BlockSpec(memory_space=pltpu.VMEM)
    return pl.pallas_call(
        functools.partial(finish_kernel, scale=scale),
        in_specs=[pl.BlockSpec(memory_space=pltpu.SMEM), vmem, vmem, vmem],
        out_specs=[vmem, vmem],
        out_shape=[
            jax.ShapeDtypeStruct((NK * half, 128), F32),
            jax.ShapeDtypeStruct((NK * peers, BLOCK_ROWS), BF16),
        ],
        compiler_params=params(4),
        name="finish",
    )(k, mine, other, everything)


def x_parts(values):
    return [lax.ppermute(values, "cent", x_perm(s)) for s in (1, 3, 2)]


def plane_exchange(blocks):
    groups = [[(z * NY + y) * NK + k for z in range(NZ) for y in range(NY)] for k in range(NK)]
    return lax.all_to_all(
        blocks, "rows", split_axis=0, concat_axis=0, tiled=True, axis_index_groups=groups
    )


def local(embeddings, centroids, owners, live_blocks):
    x = lax.axis_index("cent")
    row_place = lax.axis_index("rows")
    k = row_place & (NK - 1)
    y = (row_place // NK) & (NY - 1)
    z = row_place // (NK * NY)
    n_cent, d = centroids.shape
    half = n_cent // NK
    rows = embeddings.shape[0]
    peers = NZ * NY * NK
    total = n_cent * NX

    core = k.reshape(1).astype(jnp.int32)
    own, mine = unit_cents(core, centroids)
    right = lax.ppermute(mine, "cent", x_perm(1))
    left = lax.ppermute(mine, "cent", x_perm(-1))
    embeddings, mine = lax.optimization_barrier((embeddings, mine))
    outgoing, scaled = unit_rows(owners, live_blocks, embeddings, peers)
    arrived = lax.all_to_all(outgoing, "rows", split_axis=0, concat_axis=0, tiled=True)
    right, left, scaled = lax.optimization_barrier((right, left, scaled))
    swap = rows_perm(0, 0, 1)
    far = [lax.ppermute(t, "cent", x_perm(s)) for t, s in zip(forward_parts(right, left), (1, -1))]
    right = [right, lax.ppermute(right, "rows", swap)]
    left = [left, lax.ppermute(left, "rows", swap)]
    sums_own = first_sweep(scaled, [own])
    sums_right = first_sweep(scaled, right)
    sums_left = first_sweep(scaled, left)
    far, sums_own, sums_right, sums_left = lax.optimization_barrier(
        (far, sums_own, sums_right, sums_left)
    )
    far += [lax.ppermute(t, "rows", swap) for t in far]
    sums_far = first_sweep(scaled, far[:2])

    def line(dx, kk, quarter):
        return (((x + dx) & (NX - 1)) * n_cent + kk * half + quarter * TILE) // 128

    starts = [line(0, q // 2, q % 2) for q in range(4)]
    for dx in (-1, 1, 2):
        starts += [line(dx, k, 0), line(dx, k, 1), line(dx, 1 - k, 0), line(dx, 1 - k, 1)]
    lines = total // 128
    offsets = jnp.stack(starts).astype(jnp.int32) ^ (k * (lines // NK)).astype(jnp.int32)

    ready = [*sums_own, *sums_right, *sums_left, *sums_far]
    keep, give = last_sweep(offsets, scaled, far[2:], ready)
    keep = keep + lax.ppermute(give, "rows", swap)
    for part in x_parts(keep):
        keep = keep + part
    keep, arrived = lax.optimization_barrier((keep, arrived))
    keep = sum_blocks(plane_exchange(jnp.broadcast_to(keep[None], (NZ * NY, *keep.shape))))
    other = lax.ppermute(keep, "rows", swap)

    ratio = float(rows * NX * peers) / total
    pieces = [own, right[0], in_hbm(right[1]), left[0], in_hbm(left[1]), *far]
    targets = ((owners ^ k) & (NK - 1)) * (NZ * NY) + owners // NK
    column, sent, give, moved = second_sweep(
        offsets, targets, live_blocks, scaled, keep, other, arrived, pieces, ratio
    )
    got = lax.ppermute(give, "rows", swap)
    column = column + got[: column.shape[0]]
    everything = plane_exchange(pack(core, column, x_parts(column), sent, got))
    column = everything[:, : column.shape[0]].sum(0)
    other = lax.ppermute(column, "rows", swap)
    balance, moved_score = finish(core, column, other, everything, 1.0 / ratio)
    return moved.reshape(peers * BLOCK_ROWS, d), moved_score.reshape(-1), balance.reshape(-1)


def solution(mesh):
    placed = (P(("rows", "cent"), None), P("cent", None), P(("rows", "cent")), P(("rows", "cent")))
    return jax.shard_map(
        local,
        mesh=mesh,
        in_specs=placed,
        out_specs=(P(("rows", "cent"), None), P(("rows", "cent")), P()),
        check_vma=False,
    )
```

```python
import functools
import math

import jax
import jax.numpy as jnp
from jax import lax
from jax.experimental import pallas as pl
from jax.experimental.pallas import tpu as pltpu
from jax.sharding import PartitionSpec as P

BLOCK_ROWS = 128
SCALE = 50.0
EPSILON = 1e-06
LOG2E = math.log2(math.e)
NT = (((1,), (1,)), ((), ()))
NN = (((1,), (0,)), ((), ()))
F32, BF16 = jnp.float32, jnp.bfloat16
NX, NY, NZ, NK = 4, 4, 4, 2
TILE = 512
ROW_TILE = 512
MIB = 2**20


def params(mib):
    return pltpu.CompilerParams(vmem_limit_bytes=mib * MIB)


def in_hbm(x):
    return pltpu.with_memory_space_constraint(x, pltpu.HBM)


def in_vmem(x):
    return pltpu.with_memory_space_constraint(x, pltpu.VMEM)


def cost(rows, cents, passes):
    return pl.CostEstimate(flops=passes * rows, transcendentals=0, bytes_accessed=cents)


def x_perm(shift):
    return [(i, (i + shift) % NX) for i in range(NX)]


def rows_perm(dz, dy, dk):
    out = []
    for z in range(NZ):
        for y in range(NY):
            for k in range(NK):
                target = ((z + dz) % NZ * NY + (y + dy) % NY) * NK + (k + dk) % NK
                out.append(((z * NY + y) * NK + k, target))
    return out


def unit_f32(values):
    squares = jnp.sum(values * values, axis=-1, keepdims=True)
    return values * lax.rsqrt(squares + EPSILON)


def cents_kernel(place_ref, c_ref, all_ref, half_ref, buf, sems):
    half = buf.shape[1]
    copies = []
    for i in range(NK):
        start = pl.multiple_of((place_ref[1] ^ i) * half, half)
        copies.append(pltpu.make_async_copy(c_ref.at[pl.ds(start, half), :], buf.at[i], sems.at[i]))
    for copy in copies:
        copy.start()
    for i, copy in enumerate(copies):
        copy.wait()
        unit = unit_f32(buf[i]).astype(BF16)
        all_ref[pl.ds(pl.multiple_of((place_ref[1] ^ i) * half, half), half), :] = unit
        if i == 0:
            half_ref[...] = unit


def unit_cents(place, centroids):
    n, d = centroids.shape
    half = n // NK
    vmem = pl.BlockSpec(memory_space=pltpu.VMEM)
    return pl.pallas_call(
        cents_kernel,
        in_specs=[pl.BlockSpec(memory_space=pltpu.SMEM), pl.BlockSpec(memory_space=pltpu.HBM)],
        out_specs=[vmem, vmem],
        out_shape=[pltpu.VMEM((n, d), BF16), pltpu.VMEM((half, d), BF16)],
        scratch_shapes=[pltpu.VMEM((NK, half, d), F32), pltpu.SemaphoreType.DMA((NK,))],
        compiler_params=params(8),
        name="unit_cents",
    )(place, in_hbm(centroids))


def forward_kernel(right_ref, left_ref, first_ref, second_ref):
    n = first_ref.shape[0]
    first_ref[...] = right_ref[:n, :]
    second_ref[...] = left_ref[n:, :]


def forward_parts(right, left):
    n, d = right.shape
    vmem = pl.BlockSpec(memory_space=pltpu.VMEM)
    return pl.pallas_call(
        forward_kernel,
        in_specs=[vmem, vmem],
        out_specs=[vmem, vmem],
        out_shape=[jax.ShapeDtypeStruct((n // 2, d), BF16)] * 2,
        compiler_params=params(8),
        cost_estimate=cost(2**26, 0, 2**11),
        name="forward_parts",
    )(right, left)


def rows_kernel(owner_ref, live_ref, e_ref, out_ref, scaled_ref):
    step = pl.program_id(0)

    @pl.when(step == 0)
    def _():
        out_ref[...] = jnp.zeros_like(out_ref)

    unit = unit_f32(e_ref[...])
    scaled_ref[...] = (unit * (SCALE * LOG2E)).astype(BF16)
    low = unit.astype(BF16)
    count = e_ref.shape[0] // BLOCK_ROWS
    for b in range(count):
        block = step * count + b

        @pl.when(block < live_ref[0])
        def _():
            out_ref[owner_ref[block]] = low[b * BLOCK_ROWS : (b + 1) * BLOCK_ROWS]


def unit_rows(owners, live, embeddings, peers):
    n, d = embeddings.shape
    steps = 4
    return pl.pallas_call(
        rows_kernel,
        grid_spec=pltpu.PrefetchScalarGridSpec(
            num_scalar_prefetch=2,
            grid=(steps,),
            in_specs=[pl.BlockSpec((n // steps, d), lambda i, o, l: (i, 0))],
            out_specs=[
                pl.BlockSpec((peers, BLOCK_ROWS, d), lambda i, o, l: (0, 0, 0)),
                pl.BlockSpec((n // steps, d), lambda i, o, l: (i, 0)),
            ],
        ),
        out_shape=[pltpu.HBM((peers, BLOCK_ROWS, d), BF16), pltpu.VMEM((n, d), BF16)],
        compiler_params=params(8),
        name="unit_rows",
    )(owners, live, embeddings)


def column_sums(r_ref, c_ref, w_ref, at, tr):
    n = c_ref.shape[0]
    tc = min(TILE, n)
    out = []
    for c in range(0, n, tc):
        cents = c_ref[c : c + tc, :]
        total = jnp.zeros((8, tc), F32)
        for i in range(0, r_ref.shape[0], tr):
            p = lax.dot_general(r_ref[i : i + tr, :], cents, NT, preferred_element_type=F32)
            weights = jnp.exp2(p)
            w_ref[i : i + tr, at + c : at + c + tc] = weights.astype(BF16)
            total = total + weights.reshape(tr // 8, 8, tc).sum(0)
        out.append(jnp.sum(total, axis=0, keepdims=True))
    return out


def first_kernel(r_ref, *refs):
    pieces, (o_ref, w_ref) = refs[:-2], refs[-2:]
    at = 0
    for c_ref in pieces:
        for part in column_sums(r_ref, c_ref, w_ref, at, 256):
            o_ref[:, at : at + part.shape[1]] = part
            at += part.shape[1]


def first_sweep(scaled, pieces):
    total = sum(p.shape[0] for p in pieces)
    return pl.pallas_call(
        first_kernel,
        out_shape=[pltpu.VMEM((1, total), F32), pltpu.VMEM((scaled.shape[0], total), BF16)],
        compiler_params=params(8),
        cost_estimate=cost(scaled.shape[0], total, 1),
        name="first_sweep",
    )(in_vmem(scaled), *[in_vmem(p) for p in pieces])


def tile_lines(place_ref, lines):
    x, k = place_ref[0], place_ref[1]
    shard = lines // NX
    half = shard // NK
    out = []
    for dx in (0, -1, 1, 2):
        start = ((x + dx) & (NX - 1)) * shard
        for kk in (0, 1) if dx == 0 else (k, 1 - k):
            for quarter in range(0, half, TILE // 128):
                out.append((start + kk * half + quarter) ^ (k * (lines // NK)))
    return out


def last_kernel(place_ref, r_ref, *refs, n_new):
    pieces, ready, (keep_ref, give_ref, w_ref, buf) = refs[:n_new], refs[n_new:-4], refs[-4:]
    parts = [ref[:, j : j + TILE] for ref in ready for j in range(0, ref.shape[1], TILE)]
    at = 0
    for c_ref in pieces:
        parts += column_sums(r_ref, c_ref, w_ref, at, 256)
        at += c_ref.shape[0]
    for at, part in zip(tile_lines(place_ref, buf.shape[0]), parts):
        for j in range(TILE // 128):
            buf[pl.ds(at + j, 1), :] = part[:, j * 128 : (j + 1) * 128]
    half = keep_ref.shape[0]
    keep_ref[...] = buf[:half, :]
    give_ref[...] = buf[half:, :]


def last_sweep(place, scaled, pieces, ready):
    new = sum(p.shape[0] for p in pieces)
    total = new + sum(p.shape[1] for p in ready)
    vmem = pl.BlockSpec(memory_space=pltpu.VMEM)
    half = total // 128 // NK
    return pl.pallas_call(
        functools.partial(last_kernel, n_new=len(pieces)),
        in_specs=[pl.BlockSpec(memory_space=pltpu.SMEM)] + [vmem] * (1 + len(pieces) + len(ready)),
        out_specs=[vmem] * 3,
        out_shape=[pltpu.VMEM((half, 128), F32)] * 2
        + [pltpu.VMEM((scaled.shape[0], new), BF16)],
        scratch_shapes=[pltpu.VMEM((NK * half, 128), F32)],
        compiler_params=params(8),
        cost_estimate=cost(scaled.shape[0], new, 1),
        name="last_sweep",
    )(place, *[in_vmem(p) for p in (scaled, *pieces, *ready)])


def lane_sum(x):
    parts = [x[:, j : j + 128] for j in range(0, x.shape[1], 128)]
    while len(parts) > 1:
        parts = [parts[i] + parts[i + 1] for i in range(0, len(parts), 2)]
    return parts[0]


def second_kernel(
    place_ref, owner_ref, live_ref, r_ref, mine_ref, other_ref, *refs, n_pieces, n_weights, tr, ratio
):
    pieces, stored = refs[:n_pieces], refs[n_pieces : n_pieces + n_weights]
    keep_ref, sent_ref, give_ref, *scratch = refs[n_pieces + n_weights :]
    line_scr, score_scr, b_scr, low_scr, s_scr, i_scr = scratch
    rows = r_ref.shape[0]
    cents = [ref.at[j : j + TILE] for ref in pieces for j in range(0, ref.shape[0], TILE)]
    tiles = [(ref, j) for ref in stored for j in range(0, ref.shape[1], TILE)]
    starts = tile_lines(place_ref, line_scr.shape[0])
    lanes = TILE // 128
    half = mine_ref.shape[0]
    line_scr[:half, :] = ratio / mine_ref[...]
    line_scr[half:, :] = ratio / other_ref[...]
    for i in range(len(tiles)):
        for j in range(lanes):
            at = (i * lanes + j) * 128
            b_scr[:, at : at + 128] = line_scr[pl.ds(starts[i] + j, 1), :]
    low_scr[...] = jnp.broadcast_to(b_scr[...], low_scr.shape).astype(BF16)
    width = 256
    rg = 16

    def body(t, carry):
        row = pl.multiple_of(t * tr, tr)
        mixed = jnp.zeros((tr, r_ref.shape[1]), F32)
        for i, (ref, j) in enumerate(tiles):
            here = slice(i * TILE, (i + 1) * TILE)
            e = ref[pl.ds(row, tr), j : j + TILE] * low_scr[0:1, here]
            for g in range(0, tr, rg):
                part = lane_sum(e[g : g + rg].astype(F32))
                if i == 0:
                    s_scr[g : g + rg] = part
                else:
                    s_scr[g : g + rg] += part
            mixed = mixed + lax.dot_general(e, cents[i][...], NN, preferred_element_type=F32)
        weighted = lane_sum(mixed * r_ref[pl.ds(row, tr), :].astype(F32))
        for g in range(0, tr, width):
            inverse = 1.0 / jnp.sum(s_scr[g : g + width].T, axis=0, keepdims=True)
            score = jnp.sum(weighted[g : g + width].T, axis=0, keepdims=True) * inverse
            score_scr[pl.ds(t * (tr // width) + g // width, 1), :] = score * (1.0 / LOG2E)
            high = inverse.astype(BF16)
            low = (inverse - high.astype(F32)).astype(BF16)
            i_scr[:, pl.ds(pl.multiple_of(row + g, width), width)] = jnp.concatenate(
                [high, low, jnp.zeros((14, width), BF16)], axis=0
            )
        return carry

    lax.fori_loop(0, rows // tr, body, 0)
    for i, (ref, j) in enumerate(tiles):
        part = lax.dot_general(i_scr[...], ref[:, j : j + TILE], NN, preferred_element_type=F32)
        line = (part[0:1] + part[1:2]) * b_scr[:, i * TILE : (i + 1) * TILE]
        for j in range(lanes):
            line_scr[pl.ds(starts[i] + j, 1), :] = line[:, j * 128 : (j + 1) * 128]
    keep_ref[...] = line_scr[:half, :]
    give_ref[:half, :] = line_scr[half:, :]
    blocks = rows // BLOCK_ROWS
    peers = NZ * NY
    line_scr[: NK * peers, :] = jnp.zeros((NK * peers, BLOCK_ROWS), F32)
    for b in range(blocks):
        at = b % 2 * BLOCK_ROWS

        @pl.when(b < live_ref[0])
        def _():
            score = score_scr[b // 2 : b // 2 + 1, at : at + BLOCK_ROWS]
            owner = owner_ref[b]
            to = ((owner ^ place_ref[1]) & (NK - 1)) * peers + (owner >> 1)
            line_scr[pl.ds(to, 1), :] = score.astype(BF16).astype(F32)

    sent_ref[...] = line_scr[:peers, :]
    give_ref[half:, :] = line_scr[peers : NK * peers, :]


def second_sweep(place, owners, live, scaled, mine, other, pieces, weights, ratio):
    rows = scaled.shape[0]
    total = sum(p.shape[0] for p in pieces)
    tr = ROW_TILE
    half = mine.shape[0]
    peers = NZ * NY
    vmem = pl.BlockSpec(memory_space=pltpu.VMEM)
    smem = pl.BlockSpec(memory_space=pltpu.SMEM)
    kernel = functools.partial(
        second_kernel, n_pieces=len(pieces), n_weights=len(weights), tr=tr, ratio=ratio
    )
    return pl.pallas_call(
        kernel,
        in_specs=[smem] * 3 + [vmem] * (3 + len(pieces) + len(weights)),
        out_specs=[vmem, vmem, vmem],
        out_shape=[
            pltpu.VMEM((half, 128), F32),
            pltpu.VMEM((peers, BLOCK_ROWS), F32),
            pltpu.VMEM((half + peers, 128), F32),
        ],
        scratch_shapes=[
            pltpu.VMEM((total // 128, 128), F32),
            pltpu.VMEM((rows // 256, 256), F32),
            pltpu.VMEM((1, total), F32),
            pltpu.VMEM((16, total), BF16),
            pltpu.VMEM((tr, 128), F32),
            pltpu.VMEM((16, rows), BF16),
        ],
        compiler_params=params(10),
        cost_estimate=cost(rows, total, 3),
        name="second_sweep",
    )(
        place,
        owners,
        live,
        in_vmem(scaled),
        mine,
        other,
        *[in_vmem(p) for p in pieces],
        *[in_vmem(w) for w in weights],
    )


def place_kernel(in_ref, out_ref, buf, sems):
    steps = sems.shape[1]
    size = in_ref.shape[0] // steps
    loads, stores = [], []
    for i in range(steps):
        part = pl.ds(i * size, size)
        loads.append(pltpu.make_async_copy(in_ref.at[part], buf.at[part], sems.at[0, i]))
        stores.append(pltpu.make_async_copy(buf.at[part], out_ref.at[part], sems.at[1, i]))
        loads[-1].start()
    for load, store in zip(loads, stores):
        load.wait()
        store.start()
    for store in stores:
        store.wait()


def place_rows(arrived):
    return pl.pallas_call(
        place_kernel,
        in_specs=[pl.BlockSpec(memory_space=pl.ANY)],
        out_specs=pl.BlockSpec(memory_space=pl.ANY),
        out_shape=pltpu.HBM(arrived.shape, BF16),
        scratch_shapes=[pltpu.VMEM(arrived.shape, BF16), pltpu.SemaphoreType.DMA((2, 4))],
        compiler_params=params(8),
        cost_estimate=pl.CostEstimate(flops=0, transcendentals=0, bytes_accessed=2**23),
        name="place_rows",
    )(in_hbm(arrived))


def pack_kernel(k_ref, col_ref, a_ref, b_ref, c_ref, sent_ref, got_ref, out_ref):
    half = col_ref.shape[0]
    peers = sent_ref.shape[0]
    out_ref[:, :half, :] = jnp.broadcast_to(
        (col_ref[...] + a_ref[...] + (b_ref[...] + c_ref[...]))[None], (peers, half, 128)
    )
    out_ref[:, half:, :] = jnp.zeros((peers, out_ref.shape[1] - half, 128), F32)
    k = k_ref[1]
    for i in range(peers):
        out_ref[i, pl.ds(half + k, 1), :] = sent_ref[i : i + 1, :]
        out_ref[i, pl.ds(half + 1 - k, 1), :] = got_ref[half + i : half + i + 1, :]


def pack(k, column, arrived, sent, got):
    half, peers = column.shape[0], sent.shape[0]
    vmem = pl.BlockSpec(memory_space=pltpu.VMEM)
    return pl.pallas_call(
        pack_kernel,
        in_specs=[pl.BlockSpec(memory_space=pltpu.SMEM)] + [vmem] * 6,
        out_specs=vmem,
        out_shape=jax.ShapeDtypeStruct((peers, half + 8, 128), F32),
        compiler_params=params(4),
        name="pack",
    )(k, column, *arrived, sent, got)


def finish_kernel(k_ref, mine_ref, other_ref, all_ref, bal_ref, out_ref, *, scale):
    half = mine_ref.shape[0]
    k = k_ref[1]
    bal_ref[pl.ds(pl.multiple_of(k * half, half), half), :] = mine_ref[...] * scale
    bal_ref[pl.ds(pl.multiple_of((1 - k) * half, half), half), :] = other_ref[...] * scale
    peers = all_ref.shape[0]
    scores = jnp.concatenate([all_ref[i, half : half + NK, :] for i in range(peers)], axis=0)
    out_ref[...] = scores.astype(BF16)


def finish(k, mine, other, everything, scale):
    half, peers = mine.shape[0], everything.shape[0]
    vmem = pl.BlockSpec(memory_space=pltpu.VMEM)
    return pl.pallas_call(
        functools.partial(finish_kernel, scale=scale),
        in_specs=[pl.BlockSpec(memory_space=pltpu.SMEM), vmem, vmem, vmem],
        out_specs=[vmem, vmem],
        out_shape=[
            jax.ShapeDtypeStruct((NK * half, 128), F32),
            jax.ShapeDtypeStruct((NK * peers, BLOCK_ROWS), BF16),
        ],
        compiler_params=params(4),
        name="finish",
    )(k, mine, other, everything)


def x_parts(values):
    return [lax.ppermute(values, "cent", x_perm(s)) for s in (1, 3, 2)]


def plane_exchange(blocks):
    groups = [[(z * NY + y) * NK + k for z in range(NZ) for y in range(NY)] for k in range(NK)]
    return lax.all_to_all(
        blocks, "rows", split_axis=0, concat_axis=0, tiled=True, axis_index_groups=groups
    )


def local(embeddings, centroids, owners, live_blocks):
    x = lax.axis_index("cent")
    row_place = lax.axis_index("rows")
    k = row_place & (NK - 1)
    n_cent, d = centroids.shape
    half = n_cent // NK
    rows = embeddings.shape[0]
    peers = NZ * NY * NK
    total = n_cent * NX

    place = jnp.stack([x, k]).astype(jnp.int32)
    own, mine = unit_cents(place, centroids)
    right = lax.ppermute(mine, "cent", x_perm(1))
    left = lax.ppermute(mine, "cent", x_perm(-1))
    embeddings, mine = lax.optimization_barrier((embeddings, mine))
    outgoing, scaled = unit_rows(owners, live_blocks, embeddings, peers)
    arrived = lax.all_to_all(outgoing, "rows", split_axis=0, concat_axis=0, tiled=True)
    right, left, scaled = lax.optimization_barrier((right, left, scaled))
    swap = rows_perm(0, 0, 1)
    far = [lax.ppermute(t, "cent", x_perm(s)) for t, s in zip(forward_parts(right, left), (1, -1))]
    right = [right, lax.ppermute(right, "rows", swap)]
    left = [left, lax.ppermute(left, "rows", swap)]
    sums_own, w_own = first_sweep(scaled, [own])
    sums_right, w_right = first_sweep(scaled, right)
    sums_left, w_left = first_sweep(scaled, left)
    far, sums_own, sums_right, sums_left = lax.optimization_barrier(
        (far, sums_own, sums_right, sums_left)
    )
    far += [lax.ppermute(t, "rows", swap) for t in far]
    sums_far, w_far = first_sweep(scaled, far[:2])

    ready = [sums_own, sums_right, sums_left, sums_far]
    keep, give, w_last = last_sweep(place, scaled, far[2:], ready)
    keep = keep + lax.ppermute(give, "rows", swap)
    for part in x_parts(keep):
        keep = keep + part
    for dz, dy in ((0, 1), (1, 0)):
        for part in [lax.ppermute(keep, "rows", rows_perm(dz * s, dy * s, 0)) for s in (1, 3, 2)]:
            keep = keep + part
    other = lax.ppermute(keep, "rows", swap)

    ratio = float(rows * NX * peers) / total
    pieces = [own, *right, *left, *far]
    weights = [w_own, w_right, w_left, w_far, w_last]
    column, sent, give = second_sweep(
        place, owners, live_blocks, scaled, keep, other, pieces, weights, ratio
    )
    sent, arrived = lax.optimization_barrier((sent, arrived))
    moved = place_rows(arrived)
    sent, moved = lax.optimization_barrier((sent, moved))
    got = lax.ppermute(give, "rows", swap)
    column = column + got[: column.shape[0]]
    everything = plane_exchange(pack(place, column, x_parts(column), sent, got))
    column = everything[:, : column.shape[0]].sum(0)
    other = lax.ppermute(column, "rows", swap)
    balance, moved_score = finish(place, column, other, everything, 1.0 / ratio)
    return moved.reshape(peers * BLOCK_ROWS, d), moved_score.reshape(-1), balance.reshape(-1)


def solution(mesh):
    placed = (P(("rows", "cent"), None), P("cent", None), P(("rows", "cent")), P(("rows", "cent")))
    return jax.shard_map(
        local,
        mesh=mesh,
        in_specs=placed,
        out_specs=(P(("rows", "cent"), None), P(("rows", "cent")), P()),
        check_vma=False,
    )
```

```python
import functools
import math

import jax
import jax.numpy as jnp
from jax import lax
from jax.experimental import pallas as pl
from jax.experimental.pallas import tpu as pltpu
from jax.sharding import PartitionSpec as P

BLOCK_ROWS = 128
SCALE = 50.0
EPSILON = 1e-06
LOG2E = math.log2(math.e)
NT = (((1,), (1,)), ((), ()))
NN = (((1,), (0,)), ((), ()))
F32, BF16 = jnp.float32, jnp.bfloat16
NX, NY, NZ, NK = 4, 4, 4, 2
TILE = 512
ROW_TILE = 512
MIB = 2**20


def params(mib):
    return pltpu.CompilerParams(vmem_limit_bytes=mib * MIB)


def in_hbm(x):
    return pltpu.with_memory_space_constraint(x, pltpu.HBM)


def in_vmem(x):
    return pltpu.with_memory_space_constraint(x, pltpu.VMEM)


def cost(rows, cents, passes):
    return pl.CostEstimate(flops=passes * rows, transcendentals=0, bytes_accessed=cents)


def x_perm(shift):
    return [(i, (i + shift) % NX) for i in range(NX)]


def rows_perm(dz, dy, dk):
    out = []
    for z in range(NZ):
        for y in range(NY):
            for k in range(NK):
                target = ((z + dz) % NZ * NY + (y + dy) % NY) * NK + (k + dk) % NK
                out.append(((z * NY + y) * NK + k, target))
    return out


def unit_f32(values):
    squares = jnp.sum(values * values, axis=-1, keepdims=True)
    return values * lax.rsqrt(squares + EPSILON)


def cents_kernel(place_ref, c_ref, all_ref, half_ref, buf, sems):
    half = buf.shape[1]
    copies = []
    for i in range(NK):
        start = pl.multiple_of(((place_ref[0] & 1) ^ i) * half, half)
        copies.append(pltpu.make_async_copy(c_ref.at[pl.ds(start, half), :], buf.at[i], sems.at[i]))
    for copy in copies:
        copy.start()
    for i, copy in enumerate(copies):
        copy.wait()
        unit = unit_f32(buf[i]).astype(BF16)
        all_ref[pl.ds(pl.multiple_of(((place_ref[0] & 1) ^ i) * half, half), half), :] = unit
        if i == 0:
            half_ref[...] = unit


def unit_cents(place, centroids):
    n, d = centroids.shape
    half = n // NK
    vmem = pl.BlockSpec(memory_space=pltpu.VMEM)
    return pl.pallas_call(
        cents_kernel,
        in_specs=[pl.BlockSpec(memory_space=pltpu.SMEM), pl.BlockSpec(memory_space=pltpu.HBM)],
        out_specs=[vmem, vmem],
        out_shape=[pltpu.VMEM((n, d), BF16), pltpu.VMEM((half, d), BF16)],
        scratch_shapes=[pltpu.VMEM((NK, half, d), F32), pltpu.SemaphoreType.DMA((NK,))],
        compiler_params=params(8),
        name="unit_cents",
    )(place, in_hbm(centroids))


def forward_kernel(right_ref, left_ref, first_ref, second_ref):
    n = first_ref.shape[0]
    first_ref[...] = right_ref[:n, :]
    second_ref[...] = left_ref[n:, :]


def forward_parts(right, left):
    n, d = right.shape
    vmem = pl.BlockSpec(memory_space=pltpu.VMEM)
    return pl.pallas_call(
        forward_kernel,
        in_specs=[vmem, vmem],
        out_specs=[vmem, vmem],
        out_shape=[jax.ShapeDtypeStruct((n // 2, d), BF16)] * 2,
        compiler_params=params(8),
        cost_estimate=cost(2**26, 0, 2**11),
        name="forward_parts",
    )(right, left)


def rows_kernel(owner_ref, live_ref, e_ref, out_ref, scaled_ref, buf, sems):
    steps = sems.shape[0]
    size = buf.shape[0] // steps
    copies = []
    for i in range(steps):
        part = pl.ds(i * size, size)
        copies.append(pltpu.make_async_copy(e_ref.at[part, :], buf.at[part, :], sems.at[i]))
        copies[-1].start()
    out_ref[...] = jnp.zeros_like(out_ref)
    for i, copy in enumerate(copies):
        copy.wait()
        unit = unit_f32(buf[i * size : (i + 1) * size, :])
        scaled_ref[i * size : (i + 1) * size, :] = (unit * (SCALE * LOG2E)).astype(BF16)
        low = unit.astype(BF16)
        for b in range(size // BLOCK_ROWS):
            block = i * (size // BLOCK_ROWS) + b

            @pl.when(block < live_ref[0])
            def _():
                out_ref[owner_ref[block]] = low[b * BLOCK_ROWS : (b + 1) * BLOCK_ROWS]


def unit_rows(owners, live, embeddings, peers):
    n, d = embeddings.shape
    vmem = pl.BlockSpec(memory_space=pltpu.VMEM)
    smem = pl.BlockSpec(memory_space=pltpu.SMEM)
    whole = pl.BlockSpec((peers, BLOCK_ROWS, d), lambda: (0, 0, 0))
    return pl.pallas_call(
        rows_kernel,
        in_specs=[smem, smem, pl.BlockSpec(memory_space=pl.ANY)],
        out_specs=[whole, vmem],
        out_shape=[pltpu.HBM((peers, BLOCK_ROWS, d), BF16), pltpu.VMEM((n, d), BF16)],
        scratch_shapes=[pltpu.VMEM((n, d), F32), pltpu.SemaphoreType.DMA((4,))],
        compiler_params=params(10),
        name="unit_rows",
    )(owners, live, in_hbm(embeddings))


def column_sums(r_ref, c_ref, w_ref, at, tr):
    n = c_ref.shape[0]
    tc = min(TILE, n)
    out = []
    for c in range(0, n, tc):
        cents = c_ref[c : c + tc, :]
        total = jnp.zeros((8, tc), F32)
        for i in range(0, r_ref.shape[0], tr):
            p = lax.dot_general(r_ref[i : i + tr, :], cents, NT, preferred_element_type=F32)
            weights = jnp.exp2(p)
            w_ref[i : i + tr, at + c : at + c + tc] = weights.astype(BF16)
            total = total + weights.reshape(tr // 8, 8, tc).sum(0)
        out.append(jnp.sum(total, axis=0, keepdims=True))
    return out


def first_kernel(r_ref, *refs):
    pieces, (o_ref, w_ref) = refs[:-2], refs[-2:]
    at = 0
    for c_ref in pieces:
        for part in column_sums(r_ref, c_ref, w_ref, at, 256):
            o_ref[:, at : at + part.shape[1]] = part
            at += part.shape[1]


def first_sweep(scaled, pieces):
    total = sum(p.shape[0] for p in pieces)
    return pl.pallas_call(
        first_kernel,
        out_shape=[pltpu.VMEM((1, total), F32), pltpu.VMEM((scaled.shape[0], total), BF16)],
        compiler_params=params(8),
        cost_estimate=cost(scaled.shape[0], total, 1),
        name="first_sweep",
    )(in_vmem(scaled), *[in_vmem(p) for p in pieces])


def tile_lines(place_ref, lines):
    x, k = place_ref[0] >> 1, place_ref[0] & 1
    shard = lines // NX
    half = shard // NK
    out = []
    for dx in (0, -1, 1, 2):
        start = ((x + dx) & (NX - 1)) * shard
        for kk in (0, 1) if dx == 0 else (k, 1 - k):
            for quarter in range(0, half, TILE // 128):
                out.append((start + kk * half + quarter) ^ (k * (lines // NK)))
    return out


def last_kernel(place_ref, r_ref, *refs, n_new):
    pieces, ready, (keep_ref, give_ref, w_ref, buf) = refs[:n_new], refs[n_new:-4], refs[-4:]
    parts = [ref[:, j : j + TILE] for ref in ready for j in range(0, ref.shape[1], TILE)]
    at = 0
    for c_ref in pieces:
        parts += column_sums(r_ref, c_ref, w_ref, at, 256)
        at += c_ref.shape[0]
    for at, part in zip(tile_lines(place_ref, buf.shape[0]), parts):
        for j in range(TILE // 128):
            buf[pl.ds(at + j, 1), :] = part[:, j * 128 : (j + 1) * 128]
    half = keep_ref.shape[0]
    keep_ref[...] = buf[:half, :]
    give_ref[...] = buf[half:, :]


def last_sweep(place, scaled, pieces, ready):
    new = sum(p.shape[0] for p in pieces)
    total = new + sum(p.shape[1] for p in ready)
    vmem = pl.BlockSpec(memory_space=pltpu.VMEM)
    half = total // 128 // NK
    return pl.pallas_call(
        functools.partial(last_kernel, n_new=len(pieces)),
        in_specs=[pl.BlockSpec(memory_space=pltpu.SMEM)] + [vmem] * (1 + len(pieces) + len(ready)),
        out_specs=[vmem] * 3,
        out_shape=[pltpu.VMEM((half, 128), F32)] * 2
        + [pltpu.VMEM((scaled.shape[0], new), BF16)],
        scratch_shapes=[pltpu.VMEM((NK * half, 128), F32)],
        compiler_params=params(8),
        cost_estimate=cost(scaled.shape[0], new, 1),
        name="last_sweep",
    )(place, *[in_vmem(p) for p in (scaled, *pieces, *ready)])


def lane_sum(x):
    parts = [x[:, j : j + 128] for j in range(0, x.shape[1], 128)]
    while len(parts) > 1:
        parts = [parts[i] + parts[i + 1] for i in range(0, len(parts), 2)]
    return parts[0]


def second_kernel(
    place_ref, owner_ref, live_ref, r_ref, mine_ref, other_ref, *refs, n_pieces, n_weights, tr, ratio
):
    pieces, stored = refs[:n_pieces], refs[n_pieces : n_pieces + n_weights]
    keep_ref, sent_ref, give_ref, *scratch = refs[n_pieces + n_weights :]
    line_scr, score_scr, b_scr, low_scr, s_scr, i_scr = scratch
    rows = r_ref.shape[0]
    cents = [ref.at[j : j + TILE] for ref in pieces for j in range(0, ref.shape[0], TILE)]
    tiles = [(ref, j) for ref in stored for j in range(0, ref.shape[1], TILE)]
    starts = tile_lines(place_ref, line_scr.shape[0])
    lanes = TILE // 128
    half = mine_ref.shape[0]
    line_scr[:half, :] = ratio / mine_ref[...]
    line_scr[half:, :] = ratio / other_ref[...]
    for i in range(len(tiles)):
        for j in range(lanes):
            at = (i * lanes + j) * 128
            b_scr[:, at : at + 128] = line_scr[pl.ds(starts[i] + j, 1), :]
    low_scr[...] = jnp.broadcast_to(b_scr[...], low_scr.shape).astype(BF16)
    width = 256
    rg = 16

    def body(t, carry):
        row = pl.multiple_of(t * tr, tr)
        mixed = jnp.zeros((tr, r_ref.shape[1]), F32)
        for i, (ref, j) in enumerate(tiles):
            here = slice(i * TILE, (i + 1) * TILE)
            e = ref[pl.ds(row, tr), j : j + TILE] * low_scr[0:1, here]
            for g in range(0, tr, rg):
                part = lane_sum(e[g : g + rg].astype(F32))
                if i == 0:
                    s_scr[g : g + rg] = part
                else:
                    s_scr[g : g + rg] += part
            mixed = mixed + lax.dot_general(e, cents[i][...], NN, preferred_element_type=F32)
        weighted = lane_sum(mixed * r_ref[pl.ds(row, tr), :].astype(F32))
        for g in range(0, tr, width):
            inverse = 1.0 / jnp.sum(s_scr[g : g + width].T, axis=0, keepdims=True)
            score = jnp.sum(weighted[g : g + width].T, axis=0, keepdims=True) * inverse
            score_scr[pl.ds(t * (tr // width) + g // width, 1), :] = score * (1.0 / LOG2E)
            high = inverse.astype(BF16)
            low = (inverse - high.astype(F32)).astype(BF16)
            i_scr[:, pl.ds(pl.multiple_of(row + g, width), width)] = jnp.concatenate(
                [high, low, jnp.zeros((14, width), BF16)], axis=0
            )
        return carry

    lax.fori_loop(0, rows // tr, body, 0)
    for i, (ref, j) in enumerate(tiles):
        part = lax.dot_general(i_scr[...], ref[:, j : j + TILE], NN, preferred_element_type=F32)
        line = (part[0:1] + part[1:2]) * b_scr[:, i * TILE : (i + 1) * TILE]
        for j in range(lanes):
            line_scr[pl.ds(starts[i] + j, 1), :] = line[:, j * 128 : (j + 1) * 128]
    keep_ref[...] = line_scr[:half, :]
    give_ref[:half, :] = line_scr[half:, :]
    blocks = rows // BLOCK_ROWS
    peers = NZ * NY
    line_scr[: NK * peers, :] = jnp.zeros((NK * peers, BLOCK_ROWS), F32)
    for b in range(blocks):
        at = b % 2 * BLOCK_ROWS

        @pl.when(b < live_ref[0])
        def _():
            score = score_scr[b // 2 : b // 2 + 1, at : at + BLOCK_ROWS]
            owner = owner_ref[b]
            to = ((owner ^ place_ref[0]) & (NK - 1)) * peers + (owner >> 1)
            line_scr[pl.ds(to, 1), :] = score.astype(BF16).astype(F32)

    sent_ref[...] = line_scr[:peers, :]
    give_ref[half:, :] = line_scr[peers : NK * peers, :]


def second_sweep(place, owners, live, scaled, mine, other, pieces, weights, ratio):
    rows = scaled.shape[0]
    total = sum(p.shape[0] for p in pieces)
    tr = ROW_TILE
    half = mine.shape[0]
    peers = NZ * NY
    vmem = pl.BlockSpec(memory_space=pltpu.VMEM)
    smem = pl.BlockSpec(memory_space=pltpu.SMEM)
    kernel = functools.partial(
        second_kernel, n_pieces=len(pieces), n_weights=len(weights), tr=tr, ratio=ratio
    )
    return pl.pallas_call(
        kernel,
        in_specs=[smem] * 3 + [vmem] * (3 + len(pieces) + len(weights)),
        out_specs=[vmem, vmem, vmem],
        out_shape=[
            pltpu.VMEM((half, 128), F32),
            pltpu.VMEM((peers, BLOCK_ROWS), F32),
            pltpu.VMEM((half + peers, 128), F32),
        ],
        scratch_shapes=[
            pltpu.VMEM((total // 128, 128), F32),
            pltpu.VMEM((rows // 256, 256), F32),
            pltpu.VMEM((1, total), F32),
            pltpu.VMEM((16, total), BF16),
            pltpu.VMEM((tr, 128), F32),
            pltpu.VMEM((16, rows), BF16),
        ],
        compiler_params=params(10),
        cost_estimate=cost(rows, total, 3),
        name="second_sweep",
    )(
        place,
        owners,
        live,
        in_vmem(scaled),
        mine,
        other,
        *[in_vmem(p) for p in pieces],
        *[in_vmem(w) for w in weights],
    )


def place_kernel(in_ref, out_ref, buf, sems):
    steps = sems.shape[1]
    size = in_ref.shape[0] // steps
    loads, stores = [], []
    for i in range(steps):
        part = pl.ds(i * size, size)
        loads.append(pltpu.make_async_copy(in_ref.at[part], buf.at[part], sems.at[0, i]))
        stores.append(pltpu.make_async_copy(buf.at[part], out_ref.at[part], sems.at[1, i]))
        loads[-1].start()
    for load, store in zip(loads, stores):
        load.wait()
        store.start()
    for store in stores:
        store.wait()


def place_rows(arrived):
    return pl.pallas_call(
        place_kernel,
        in_specs=[pl.BlockSpec(memory_space=pl.ANY)],
        out_specs=pl.BlockSpec(memory_space=pl.ANY),
        out_shape=pltpu.HBM(arrived.shape, BF16),
        scratch_shapes=[pltpu.VMEM(arrived.shape, BF16), pltpu.SemaphoreType.DMA((2, 4))],
        compiler_params=params(8),
        cost_estimate=pl.CostEstimate(flops=0, transcendentals=0, bytes_accessed=2**23),
        name="place_rows",
    )(in_hbm(arrived))


def pack_kernel(k_ref, col_ref, a_ref, b_ref, c_ref, sent_ref, got_ref, out_ref):
    half = col_ref.shape[0]
    peers = sent_ref.shape[0]
    out_ref[:, :half, :] = jnp.broadcast_to(
        (col_ref[...] + a_ref[...] + (b_ref[...] + c_ref[...]))[None], (peers, half, 128)
    )
    out_ref[:, half:, :] = jnp.zeros((peers, out_ref.shape[1] - half, 128), F32)
    k = k_ref[0] & 1
    for i in range(peers):
        out_ref[i, pl.ds(half + k, 1), :] = sent_ref[i : i + 1, :]
        out_ref[i, pl.ds(half + 1 - k, 1), :] = got_ref[half + i : half + i + 1, :]


def pack(k, column, arrived, sent, got):
    half, peers = column.shape[0], sent.shape[0]
    vmem = pl.BlockSpec(memory_space=pltpu.VMEM)
    return pl.pallas_call(
        pack_kernel,
        in_specs=[pl.BlockSpec(memory_space=pltpu.SMEM)] + [vmem] * 6,
        out_specs=vmem,
        out_shape=jax.ShapeDtypeStruct((peers, half + 8, 128), F32),
        compiler_params=params(4),
        name="pack",
    )(k, column, *arrived, sent, got)


def finish_kernel(k_ref, mine_ref, other_ref, all_ref, bal_ref, out_ref, *, scale):
    half = mine_ref.shape[0]
    k = k_ref[0] & 1
    bal_ref[pl.ds(pl.multiple_of(k * half, half), half), :] = mine_ref[...] * scale
    bal_ref[pl.ds(pl.multiple_of((1 - k) * half, half), half), :] = other_ref[...] * scale
    peers = all_ref.shape[0]
    scores = jnp.concatenate([all_ref[i, half : half + NK, :] for i in range(peers)], axis=0)
    out_ref[...] = scores.astype(BF16)


def finish(k, mine, other, everything, scale):
    half, peers = mine.shape[0], everything.shape[0]
    vmem = pl.BlockSpec(memory_space=pltpu.VMEM)
    return pl.pallas_call(
        functools.partial(finish_kernel, scale=scale),
        in_specs=[pl.BlockSpec(memory_space=pltpu.SMEM), vmem, vmem, vmem],
        out_specs=[vmem, vmem],
        out_shape=[
            jax.ShapeDtypeStruct((NK * half, 128), F32),
            jax.ShapeDtypeStruct((NK * peers, BLOCK_ROWS), BF16),
        ],
        compiler_params=params(4),
        name="finish",
    )(k, mine, other, everything)


def x_parts(values):
    return [lax.ppermute(values, "cent", x_perm(s)) for s in (1, 3, 2)]


def plane_exchange(blocks):
    groups = [[(z * NY + y) * NK + k for z in range(NZ) for y in range(NY)] for k in range(NK)]
    return lax.all_to_all(
        blocks, "rows", split_axis=0, concat_axis=0, tiled=True, axis_index_groups=groups
    )


def local(embeddings, centroids, owners, live_blocks):
    x = lax.axis_index("cent")
    row_place = lax.axis_index("rows")
    k = row_place & (NK - 1)
    n_cent, d = centroids.shape
    half = n_cent // NK
    rows = embeddings.shape[0]
    peers = NZ * NY * NK
    total = n_cent * NX

    place = (x * NK + k).reshape(1).astype(jnp.int32)
    own, mine = unit_cents(place, centroids)
    right = lax.ppermute(mine, "cent", x_perm(1))
    left = lax.ppermute(mine, "cent", x_perm(-1))
    embeddings, mine = lax.optimization_barrier((embeddings, mine))
    outgoing, scaled = unit_rows(owners, live_blocks, embeddings, peers)
    arrived = lax.all_to_all(outgoing, "rows", split_axis=0, concat_axis=0, tiled=True)
    right, left, scaled = lax.optimization_barrier((right, left, scaled))
    swap = rows_perm(0, 0, 1)
    far = [lax.ppermute(t, "cent", x_perm(s)) for t, s in zip(forward_parts(right, left), (1, -1))]
    right = [right, lax.ppermute(right, "rows", swap)]
    left = [left, lax.ppermute(left, "rows", swap)]
    sums_own, w_own = first_sweep(scaled, [own])
    sums_right, w_right = first_sweep(scaled, right)
    sums_left, w_left = first_sweep(scaled, left)
    far, sums_own, sums_right, sums_left = lax.optimization_barrier(
        (far, sums_own, sums_right, sums_left)
    )
    far += [lax.ppermute(t, "rows", swap) for t in far]
    sums_far, w_far = first_sweep(scaled, far[:2])

    ready = [sums_own, sums_right, sums_left, sums_far]
    keep, give, w_last = last_sweep(place, scaled, far[2:], ready)
    keep = keep + lax.ppermute(give, "rows", swap)
    for part in x_parts(keep):
        keep = keep + part
    for dz, dy in ((0, 1), (1, 0)):
        for part in [lax.ppermute(keep, "rows", rows_perm(dz * s, dy * s, 0)) for s in (1, 3, 2)]:
            keep = keep + part
    other = lax.ppermute(keep, "rows", swap)

    ratio = float(rows * NX * peers) / total
    pieces = [own, *right, *left, *far]
    weights = [w_own, w_right, w_left, w_far, w_last]
    column, sent, give = second_sweep(
        place, owners, live_blocks, scaled, keep, other, pieces, weights, ratio
    )
    sent, arrived = lax.optimization_barrier((sent, arrived))
    moved = place_rows(arrived)
    sent, moved = lax.optimization_barrier((sent, moved))
    got = lax.ppermute(give, "rows", swap)
    column = column + got[: column.shape[0]]
    everything = plane_exchange(pack(place, column, x_parts(column), sent, got))
    column = everything[:, : column.shape[0]].sum(0)
    other = lax.ppermute(column, "rows", swap)
    balance, moved_score = finish(place, column, other, everything, 1.0 / ratio)
    return moved.reshape(peers * BLOCK_ROWS, d), moved_score.reshape(-1), balance.reshape(-1)


def solution(mesh):
    placed = (P(("rows", "cent"), None), P("cent", None), P(("rows", "cent")), P(("rows", "cent")))
    return jax.shard_map(
        local,
        mesh=mesh,
        in_specs=placed,
        out_specs=(P(("rows", "cent"), None), P(("rows", "cent")), P()),
        check_vma=False,
    )
```

```python
import functools
import math

import jax
import jax.numpy as jnp
from jax import lax
from jax.experimental import pallas as pl
from jax.experimental.pallas import tpu as pltpu
from jax.sharding import PartitionSpec as P

BLOCK_ROWS = 128
SCALE = 50.0
EPSILON = 1e-06
LOG2E = math.log2(math.e)
NT = (((1,), (1,)), ((), ()))
NN = (((1,), (0,)), ((), ()))
F32, BF16 = jnp.float32, jnp.bfloat16
NX, NY, NZ, NK = 4, 4, 4, 2
TILE = 512
ROW_TILE = 512
MIB = 2**20


def params(mib):
    return pltpu.CompilerParams(vmem_limit_bytes=mib * MIB)


def in_hbm(x):
    return pltpu.with_memory_space_constraint(x, pltpu.HBM)


def in_vmem(x):
    return pltpu.with_memory_space_constraint(x, pltpu.VMEM)


def cost(rows, cents, passes):
    return pl.CostEstimate(flops=passes * rows, transcendentals=0, bytes_accessed=cents)


def x_perm(shift):
    return [(i, (i + shift) % NX) for i in range(NX)]


def rows_perm(dz, dy, dk):
    out = []
    for z in range(NZ):
        for y in range(NY):
            for k in range(NK):
                target = ((z + dz) % NZ * NY + (y + dy) % NY) * NK + (k + dk) % NK
                out.append(((z * NY + y) * NK + k, target))
    return out


def unit_f32(values):
    squares = jnp.sum(values * values, axis=-1, keepdims=True)
    return values * lax.rsqrt(squares + EPSILON)


def cents_kernel(place_ref, c_ref, all_ref, half_ref, buf, sems):
    half = buf.shape[1]
    copies = []
    for i in range(NK):
        start = pl.multiple_of(((place_ref[0] & 1) ^ i) * half, half)
        copies.append(pltpu.make_async_copy(c_ref.at[pl.ds(start, half), :], buf.at[i], sems.at[i]))
    for copy in copies:
        copy.start()
    for i, copy in enumerate(copies):
        copy.wait()
        unit = unit_f32(buf[i]).astype(BF16)
        all_ref[pl.ds(pl.multiple_of(((place_ref[0] & 1) ^ i) * half, half), half), :] = unit
        if i == 0:
            half_ref[...] = unit


def unit_cents(place, centroids):
    n, d = centroids.shape
    half = n // NK
    vmem = pl.BlockSpec(memory_space=pltpu.VMEM)
    return pl.pallas_call(
        cents_kernel,
        in_specs=[pl.BlockSpec(memory_space=pltpu.SMEM), pl.BlockSpec(memory_space=pltpu.HBM)],
        out_specs=[vmem, vmem],
        out_shape=[pltpu.VMEM((n, d), BF16), pltpu.VMEM((half, d), BF16)],
        scratch_shapes=[pltpu.VMEM((NK, half, d), F32), pltpu.SemaphoreType.DMA((NK,))],
        compiler_params=params(8),
        name="unit_cents",
    )(place, in_hbm(centroids))


def forward_kernel(in_ref, out_ref, *, start):
    out_ref[...] = in_ref[start : start + out_ref.shape[0], :]


def forward_part(piece, start, weight):
    n, d = piece.shape
    vmem = pl.BlockSpec(memory_space=pltpu.VMEM)
    return pl.pallas_call(
        functools.partial(forward_kernel, start=start),
        in_specs=[vmem],
        out_specs=vmem,
        out_shape=jax.ShapeDtypeStruct((n // 2, d), BF16),
        compiler_params=params(8),
        cost_estimate=cost(weight, 0, 2**11),
        name="forward_part",
    )(piece)


def rows_kernel(owner_ref, live_ref, e_ref, out_ref, scaled_ref, buf, sems):
    steps = sems.shape[0]
    size = buf.shape[0] // steps
    copies = []
    for i in range(steps):
        part = pl.ds(i * size, size)
        copies.append(pltpu.make_async_copy(e_ref.at[part, :], buf.at[part, :], sems.at[i]))
        copies[-1].start()
    out_ref[...] = jnp.zeros_like(out_ref)
    for i, copy in enumerate(copies):
        copy.wait()
        unit = unit_f32(buf[i * size : (i + 1) * size, :])
        scaled_ref[i * size : (i + 1) * size, :] = (unit * (SCALE * LOG2E)).astype(BF16)
        low = unit.astype(BF16)
        for b in range(size // BLOCK_ROWS):
            block = i * (size // BLOCK_ROWS) + b

            @pl.when(block < live_ref[0])
            def _():
                out_ref[owner_ref[block]] = low[b * BLOCK_ROWS : (b + 1) * BLOCK_ROWS]


def unit_rows(owners, live, embeddings, peers):
    n, d = embeddings.shape
    vmem = pl.BlockSpec(memory_space=pltpu.VMEM)
    smem = pl.BlockSpec(memory_space=pltpu.SMEM)
    whole = pl.BlockSpec((peers, BLOCK_ROWS, d), lambda: (0, 0, 0))
    return pl.pallas_call(
        rows_kernel,
        in_specs=[smem, smem, pl.BlockSpec(memory_space=pl.ANY)],
        out_specs=[whole, vmem],
        out_shape=[pltpu.HBM((peers, BLOCK_ROWS, d), BF16), pltpu.VMEM((n, d), BF16)],
        scratch_shapes=[pltpu.VMEM((n, d), F32), pltpu.SemaphoreType.DMA((4,))],
        compiler_params=params(10),
        name="unit_rows",
    )(owners, live, in_hbm(embeddings))


def column_sums(r_ref, c_ref, w_ref, at, tr):
    n = c_ref.shape[0]
    tc = min(TILE, n)
    out = []
    for c in range(0, n, tc):
        cents = c_ref[c : c + tc, :]
        total = jnp.zeros((8, tc), F32)
        for i in range(0, r_ref.shape[0], tr):
            p = lax.dot_general(r_ref[i : i + tr, :], cents, NT, preferred_element_type=F32)
            weights = jnp.exp2(p)
            w_ref[i : i + tr, at + c : at + c + tc] = weights.astype(BF16)
            total = total + weights.reshape(tr // 8, 8, tc).sum(0)
        out.append(jnp.sum(total, axis=0, keepdims=True))
    return out


def first_kernel(r_ref, *refs):
    pieces, (o_ref, w_ref) = refs[:-2], refs[-2:]
    at = 0
    for c_ref in pieces:
        for part in column_sums(r_ref, c_ref, w_ref, at, 256):
            o_ref[:, at : at + part.shape[1]] = part
            at += part.shape[1]


def first_sweep(scaled, pieces):
    total = sum(p.shape[0] for p in pieces)
    return pl.pallas_call(
        first_kernel,
        out_shape=[pltpu.VMEM((1, total), F32), pltpu.VMEM((scaled.shape[0], total), BF16)],
        compiler_params=params(8),
        cost_estimate=cost(scaled.shape[0], total, 1),
        name="first_sweep",
    )(in_vmem(scaled), *[in_vmem(p) for p in pieces])


def tile_lines(place_ref, lines):
    x, k = place_ref[0] >> 1, place_ref[0] & 1
    shard = lines // NX
    half = shard // NK
    out = []
    for dx in (0, -1, 1, 2):
        start = ((x + dx) & (NX - 1)) * shard
        for kk in (0, 1) if dx == 0 else (k, 1 - k):
            for quarter in range(0, half, TILE // 128):
                out.append((start + kk * half + quarter) ^ (k * (lines // NK)))
    return out


def last_kernel(place_ref, r_ref, *refs, n_new):
    pieces, ready, (keep_ref, give_ref, w_ref, buf) = refs[:n_new], refs[n_new:-4], refs[-4:]
    parts = [ref[:, j : j + TILE] for ref in ready for j in range(0, ref.shape[1], TILE)]
    at = 0
    for c_ref in pieces:
        parts += column_sums(r_ref, c_ref, w_ref, at, 256)
        at += c_ref.shape[0]
    for at, part in zip(tile_lines(place_ref, buf.shape[0]), parts):
        for j in range(TILE // 128):
            buf[pl.ds(at + j, 1), :] = part[:, j * 128 : (j + 1) * 128]
    half = keep_ref.shape[0]
    keep_ref[...] = buf[:half, :]
    give_ref[...] = buf[half:, :]


def last_sweep(place, scaled, pieces, ready):
    new = sum(p.shape[0] for p in pieces)
    total = new + sum(p.shape[1] for p in ready)
    vmem = pl.BlockSpec(memory_space=pltpu.VMEM)
    half = total // 128 // NK
    return pl.pallas_call(
        functools.partial(last_kernel, n_new=len(pieces)),
        in_specs=[pl.BlockSpec(memory_space=pltpu.SMEM)] + [vmem] * (1 + len(pieces) + len(ready)),
        out_specs=[vmem] * 3,
        out_shape=[pltpu.VMEM((half, 128), F32)] * 2
        + [pltpu.VMEM((scaled.shape[0], new), BF16)],
        scratch_shapes=[pltpu.VMEM((NK * half, 128), F32)],
        compiler_params=params(8),
        cost_estimate=cost(scaled.shape[0], new, 1),
        name="last_sweep",
    )(place, *[in_vmem(p) for p in (scaled, *pieces, *ready)])


def lane_sum(x):
    parts = [x[:, j : j + 128] for j in range(0, x.shape[1], 128)]
    while len(parts) > 1:
        parts = [parts[i] + parts[i + 1] for i in range(0, len(parts), 2)]
    return parts[0]


def second_kernel(
    place_ref, owner_ref, live_ref, r_ref, mine_ref, other_ref, *refs, n_pieces, n_weights, tr, ratio
):
    pieces, stored = refs[:n_pieces], refs[n_pieces : n_pieces + n_weights]
    keep_ref, sent_ref, give_ref, *scratch = refs[n_pieces + n_weights :]
    line_scr, score_scr, b_scr, low_scr, s_scr, i_scr = scratch
    rows = r_ref.shape[0]
    cents = [ref.at[j : j + TILE] for ref in pieces for j in range(0, ref.shape[0], TILE)]
    tiles = [(ref, j) for ref in stored for j in range(0, ref.shape[1], TILE)]
    starts = tile_lines(place_ref, line_scr.shape[0])
    lanes = TILE // 128
    half = mine_ref.shape[0]
    line_scr[:half, :] = ratio / mine_ref[...]
    line_scr[half:, :] = ratio / other_ref[...]
    for i in range(len(tiles)):
        for j in range(lanes):
            at = (i * lanes + j) * 128
            b_scr[:, at : at + 128] = line_scr[pl.ds(starts[i] + j, 1), :]
    low_scr[...] = jnp.broadcast_to(b_scr[...], low_scr.shape).astype(BF16)
    width = 256
    rg = 16

    def body(t, carry):
        row = pl.multiple_of(t * tr, tr)
        mixed = jnp.zeros((tr, r_ref.shape[1]), F32)
        for i, (ref, j) in enumerate(tiles):
            here = slice(i * TILE, (i + 1) * TILE)
            e = ref[pl.ds(row, tr), j : j + TILE] * low_scr[0:1, here]
            for g in range(0, tr, rg):
                part = lane_sum(e[g : g + rg].astype(F32))
                if i == 0:
                    s_scr[g : g + rg] = part
                else:
                    s_scr[g : g + rg] += part
            mixed = mixed + lax.dot_general(e, cents[i][...], NN, preferred_element_type=F32)
        weighted = lane_sum(mixed * r_ref[pl.ds(row, tr), :].astype(F32))
        for g in range(0, tr, width):
            inverse = 1.0 / jnp.sum(s_scr[g : g + width].T, axis=0, keepdims=True)
            score = jnp.sum(weighted[g : g + width].T, axis=0, keepdims=True) * inverse
            score_scr[pl.ds(t * (tr // width) + g // width, 1), :] = score * (1.0 / LOG2E)
            high = inverse.astype(BF16)
            low = (inverse - high.astype(F32)).astype(BF16)
            i_scr[:, pl.ds(pl.multiple_of(row + g, width), width)] = jnp.concatenate(
                [high, low, jnp.zeros((14, width), BF16)], axis=0
            )
        return carry

    lax.fori_loop(0, rows // tr, body, 0)
    for i, (ref, j) in enumerate(tiles):
        part = lax.dot_general(i_scr[...], ref[:, j : j + TILE], NN, preferred_element_type=F32)
        line = (part[0:1] + part[1:2]) * b_scr[:, i * TILE : (i + 1) * TILE]
        for j in range(lanes):
            line_scr[pl.ds(starts[i] + j, 1), :] = line[:, j * 128 : (j + 1) * 128]
    keep_ref[...] = line_scr[:half, :]
    give_ref[:half, :] = line_scr[half:, :]
    blocks = rows // BLOCK_ROWS
    peers = NZ * NY
    line_scr[: NK * peers, :] = jnp.zeros((NK * peers, BLOCK_ROWS), F32)
    for b in range(blocks):
        at = b % 2 * BLOCK_ROWS

        @pl.when(b < live_ref[0])
        def _():
            score = score_scr[b // 2 : b // 2 + 1, at : at + BLOCK_ROWS]
            owner = owner_ref[b]
            to = ((owner ^ place_ref[0]) & (NK - 1)) * peers + (owner >> 1)
            line_scr[pl.ds(to, 1), :] = score.astype(BF16).astype(F32)

    sent_ref[...] = line_scr[:peers, :]
    give_ref[half:, :] = line_scr[peers : NK * peers, :]


def second_sweep(place, owners, live, scaled, mine, other, pieces, weights, ratio):
    rows = scaled.shape[0]
    total = sum(p.shape[0] for p in pieces)
    tr = ROW_TILE
    half = mine.shape[0]
    peers = NZ * NY
    vmem = pl.BlockSpec(memory_space=pltpu.VMEM)
    smem = pl.BlockSpec(memory_space=pltpu.SMEM)
    kernel = functools.partial(
        second_kernel, n_pieces=len(pieces), n_weights=len(weights), tr=tr, ratio=ratio
    )
    return pl.pallas_call(
        kernel,
        in_specs=[smem] * 3 + [vmem] * (3 + len(pieces) + len(weights)),
        out_specs=[vmem, vmem, vmem],
        out_shape=[
            pltpu.VMEM((half, 128), F32),
            pltpu.VMEM((peers, BLOCK_ROWS), F32),
            pltpu.VMEM((half + peers, 128), F32),
        ],
        scratch_shapes=[
            pltpu.VMEM((total // 128, 128), F32),
            pltpu.VMEM((rows // 256, 256), F32),
            pltpu.VMEM((1, total), F32),
            pltpu.VMEM((16, total), BF16),
            pltpu.VMEM((tr, 128), F32),
            pltpu.VMEM((16, rows), BF16),
        ],
        compiler_params=params(10),
        cost_estimate=cost(rows, total, 3),
        name="second_sweep",
    )(
        place,
        owners,
        live,
        in_vmem(scaled),
        mine,
        other,
        *[in_vmem(p) for p in pieces],
        *[in_vmem(w) for w in weights],
    )


def place_kernel(in_ref, out_ref, buf, sems):
    steps = sems.shape[1]
    size = in_ref.shape[0] // steps
    loads, stores = [], []
    for i in range(steps):
        part = pl.ds(i * size, size)
        loads.append(pltpu.make_async_copy(in_ref.at[part], buf.at[part], sems.at[0, i]))
        stores.append(pltpu.make_async_copy(buf.at[part], out_ref.at[part], sems.at[1, i]))
        loads[-1].start()
    for load, store in zip(loads, stores):
        load.wait()
        store.start()
    for store in stores:
        store.wait()


def place_rows(arrived):
    return pl.pallas_call(
        place_kernel,
        in_specs=[pl.BlockSpec(memory_space=pl.ANY)],
        out_specs=pl.BlockSpec(memory_space=pl.ANY),
        out_shape=pltpu.HBM(arrived.shape, BF16),
        scratch_shapes=[pltpu.VMEM(arrived.shape, BF16), pltpu.SemaphoreType.DMA((2, 4))],
        compiler_params=params(8),
        cost_estimate=pl.CostEstimate(flops=0, transcendentals=0, bytes_accessed=2**23),
        name="place_rows",
    )(in_hbm(arrived))


def pack_kernel(k_ref, col_ref, a_ref, b_ref, c_ref, sent_ref, got_ref, out_ref):
    half = col_ref.shape[0]
    peers = sent_ref.shape[0]
    out_ref[:, :half, :] = jnp.broadcast_to(
        (col_ref[...] + a_ref[...] + (b_ref[...] + c_ref[...]))[None], (peers, half, 128)
    )
    out_ref[:, half:, :] = jnp.zeros((peers, out_ref.shape[1] - half, 128), F32)
    k = k_ref[0] & 1
    for i in range(peers):
        out_ref[i, pl.ds(half + k, 1), :] = sent_ref[i : i + 1, :]
        out_ref[i, pl.ds(half + 1 - k, 1), :] = got_ref[half + i : half + i + 1, :]


def pack(k, column, arrived, sent, got):
    half, peers = column.shape[0], sent.shape[0]
    vmem = pl.BlockSpec(memory_space=pltpu.VMEM)
    return pl.pallas_call(
        pack_kernel,
        in_specs=[pl.BlockSpec(memory_space=pltpu.SMEM)] + [vmem] * 6,
        out_specs=vmem,
        out_shape=jax.ShapeDtypeStruct((peers, half + 8, 128), F32),
        compiler_params=params(4),
        name="pack",
    )(k, column, *arrived, sent, got)


def finish_kernel(k_ref, mine_ref, other_ref, all_ref, bal_ref, out_ref, *, scale):
    half = mine_ref.shape[0]
    k = k_ref[0] & 1
    bal_ref[pl.ds(pl.multiple_of(k * half, half), half), :] = mine_ref[...] * scale
    bal_ref[pl.ds(pl.multiple_of((1 - k) * half, half), half), :] = other_ref[...] * scale
    peers = all_ref.shape[0]
    scores = jnp.concatenate([all_ref[i, half : half + NK, :] for i in range(peers)], axis=0)
    out_ref[...] = scores.astype(BF16)


def finish(k, mine, other, everything, scale):
    half, peers = mine.shape[0], everything.shape[0]
    vmem = pl.BlockSpec(memory_space=pltpu.VMEM)
    return pl.pallas_call(
        functools.partial(finish_kernel, scale=scale),
        in_specs=[pl.BlockSpec(memory_space=pltpu.SMEM), vmem, vmem, vmem],
        out_specs=[vmem, vmem],
        out_shape=[
            jax.ShapeDtypeStruct((NK * half, 128), F32),
            jax.ShapeDtypeStruct((NK * peers, BLOCK_ROWS), BF16),
        ],
        compiler_params=params(4),
        name="finish",
    )(k, mine, other, everything)


def x_parts(values):
    return [lax.ppermute(values, "cent", x_perm(s)) for s in (1, 3, 2)]


def plane_exchange(blocks):
    groups = [[(z * NY + y) * NK + k for z in range(NZ) for y in range(NY)] for k in range(NK)]
    return lax.all_to_all(
        blocks, "rows", split_axis=0, concat_axis=0, tiled=True, axis_index_groups=groups
    )


def local(embeddings, centroids, owners, live_blocks):
    x = lax.axis_index("cent")
    row_place = lax.axis_index("rows")
    k = row_place & (NK - 1)
    n_cent, d = centroids.shape
    half = n_cent // NK
    rows = embeddings.shape[0]
    peers = NZ * NY * NK
    total = n_cent * NX

    place = (x * NK + k).reshape(1).astype(jnp.int32)
    own, mine = unit_cents(place, centroids)
    right = lax.ppermute(mine, "cent", x_perm(1))
    left = lax.ppermute(mine, "cent", x_perm(-1))
    embeddings, mine = lax.optimization_barrier((embeddings, mine))
    outgoing, scaled = unit_rows(owners, live_blocks, embeddings, peers)
    arrived = lax.all_to_all(outgoing, "rows", split_axis=0, concat_axis=0, tiled=True)
    far_left = lax.ppermute(forward_part(left, half // 2, 1), "cent", x_perm(-1))
    right, left, scaled = lax.optimization_barrier((right, left, scaled))
    swap = rows_perm(0, 0, 1)
    far = [lax.ppermute(forward_part(right, 0, 2**26), "cent", x_perm(1)), far_left]
    right = [right, lax.ppermute(right, "rows", swap)]
    left = [left, lax.ppermute(left, "rows", swap)]
    sums_own, w_own = first_sweep(scaled, [own])
    sums_right, w_right = first_sweep(scaled, right)
    sums_left, w_left = first_sweep(scaled, left)
    far, sums_own, sums_right, sums_left = lax.optimization_barrier(
        (far, sums_own, sums_right, sums_left)
    )
    far += [lax.ppermute(t, "rows", swap) for t in far]
    sums_far, w_far = first_sweep(scaled, far[:2])

    ready = [sums_own, sums_right, sums_left, sums_far]
    keep, give, w_last = last_sweep(place, scaled, far[2:], ready)
    keep = keep + lax.ppermute(give, "rows", swap)
    for part in x_parts(keep):
        keep = keep + part
    for dz, dy in ((0, 1), (1, 0)):
        for part in [lax.ppermute(keep, "rows", rows_perm(dz * s, dy * s, 0)) for s in (1, 3, 2)]:
            keep = keep + part
    other = lax.ppermute(keep, "rows", swap)

    ratio = float(rows * NX * peers) / total
    pieces = [own, *right, *left, *far]
    weights = [w_own, w_right, w_left, w_far, w_last]
    column, sent, give = second_sweep(
        place, owners, live_blocks, scaled, keep, other, pieces, weights, ratio
    )
    sent, arrived = lax.optimization_barrier((sent, arrived))
    moved = place_rows(arrived)
    sent, moved = lax.optimization_barrier((sent, moved))
    got = lax.ppermute(give, "rows", swap)
    column = column + got[: column.shape[0]]
    everything = plane_exchange(pack(place, column, x_parts(column), sent, got))
    column = everything[:, : column.shape[0]].sum(0)
    other = lax.ppermute(column, "rows", swap)
    balance, moved_score = finish(place, column, other, everything, 1.0 / ratio)
    return moved.reshape(peers * BLOCK_ROWS, d), moved_score.reshape(-1), balance.reshape(-1)


def solution(mesh):
    placed = (P(("rows", "cent"), None), P("cent", None), P(("rows", "cent")), P(("rows", "cent")))
    return jax.shard_map(
        local,
        mesh=mesh,
        in_specs=placed,
        out_specs=(P(("rows", "cent"), None), P(("rows", "cent")), P()),
        check_vma=False,
    )
```
